32 devices in a mesh: vocab: 4 (over y, core), docs: 8 (over z, x).
Axes of the slice: x: 2, y: 2, z: 4, core: 2. Of those that a mesh axis runs over, the one named last changes fastest.
Arguments:
- counts: bfloat16 [4096, 4, 128], P(('vocab', 'docs')), may hold values from 0 to 2
- doc_owner: int32 [4096, 4], P(('vocab', 'docs')), may hold values from 0 to 31, all different within a row; in each aligned block of 128 rows (0 to 127, 128 to 255, ...) at most 32 rows name the same one
- doc_sub: int32 [4096, 4], P(('vocab', 'docs')), may hold values from 0 to 7
- doc_len: int32 [4096], P(('vocab', 'docs')), may hold values from 256 to 1023
- first_weight: bfloat16 [32768, 2048], P(('vocab', 'docs')), may hold values from -0.25 to 0.25
- first_bias: float32 [2048], replicated, may hold values from -3 to 3
- head_weight: bfloat16 [2048, 1536], P('vocab', 'docs'), may hold values from -0.125 to 0.125
- head_bias: float32 [1536], replicated, may hold values from -4 to 4
- factor: bfloat16 [1536, 1536], P('vocab', 'docs'), as said below
- noise_draw: bfloat16 [4096, 1536], P(('vocab', 'docs')), may hold values from -5 to 5
Outputs:
- sample: bfloat16 [4096, 1536], P(('vocab', 'docs'))
The draws below stay inside these ranges and needn't reach their ends.
Inputs may be any that keep to these rules, and one draw needn't show every extreme that they name: `doc_owner`: each document names 4 different owners. The documents of one device name one owner in at most 32 slots, and on some device some owner is named in exactly 32 slots. `factor`: lower triangular; diagonal entries lie between 0.5 and 1.5.
All inputs are finite; a program needn't handle non-finite values.
Results may differ from the reference program's by a relative error of at most 0.0038.
Values may be sent and summed in bfloat16 or wider, within the bound.
A program may use at most 128 MiB of HBM per device.

```python
import math
import jax
import jax.numpy as jnp
import numpy as np
from jax import lax

VOC_DEV = 1024
H = 2048
K = 1536
NB = 4
DOC_DEV = 128
VOCAB = 32768
NDOC = 4096
CAP = 32
DEVICES = 32


def draw_factor(key, part):
    key_diag = jax.random.fold_in(key, 11)
    key_low = jax.random.fold_in(key, 23)
    row_index = jnp.arange(K)[:, None]
    col_index = jnp.arange(K)[None, :]
    diagonal = jax.random.uniform(key_diag, (K, 1), jnp.float32, 0.5, 1.5)
    lower_vals = jax.random.normal(key_low, (K, K), jnp.float32)
    off_scale = 0.6 / jnp.sqrt(jnp.maximum(row_index, 1).astype(jnp.float32))
    lower_part = jnp.where(col_index < row_index, lower_vals * off_scale, 0.0)
    result = lower_part + jnp.where(col_index == row_index, diagonal, 0.0)
    return result.astype(jnp.bfloat16)


def touch_ends(entries, rng, least, top_value):
    longest = entries.shape.index(max(entries.shape))
    spots = []
    for shift in (0, 1):
        where = [jax.random.randint(jax.random.fold_in(rng, axis), (), 0, length) for axis, length in enumerate(entries.shape)]
        where[longest] = (where[longest] + shift) % entries.shape[longest]
        spots.append(tuple(where))
    return entries.at[spots[0]].set(least).at[spots[1]].set(top_value)


def steps_of(own_key, shape, shards, low, top_value):
    gain, own = 1.0, jax.random.fold_in(own_key, 6)
    for dim, parts in shards:
        steps = jnp.exp(jax.random.uniform(jax.random.fold_in(own, dim), (parts,), jnp.float32, low / len(shards), top_value / len(shards)))
        gain = gain * jnp.repeat(steps, shape[dim] // parts).reshape([-1 if axis == dim else 1 for axis in range(len(shape))])
    return gain


def assign_block(key, own, number, rows, amount, top, bound, lean):
    order = jax.random.permutation(key, amount)
    packed, ordinary = shares(amount, rows * top, bound, lean, True), shares(amount, rows * top, bound, lean, False)
    places = jnp.arange(amount)

    def named(sizes, turn):
        used = int((sizes > 0).sum())
        fixed = max(1, used // 4)
        shifted = fixed + (places - fixed + turn * (used - fixed)) % max(1, amount - fixed)
        return jnp.zeros((amount,), jnp.int32).at[order[jnp.where(places < fixed, places, shifted)]].set(jnp.asarray(sizes, jnp.int32))

    sizes = jnp.where(number % 4 == 0, named(packed, number // 4), named(ordinary, number - number // 4 - 1))
    mixed = jax.random.permutation(jax.random.fold_in(own, 3), amount)
    source_of, receiver = mixed[0:amount // 2 * 2:2], mixed[1:amount // 2 * 2:2]
    slack = jnp.minimum(sizes[source_of] - 1, bound - sizes[receiver]) // 2
    slack = jnp.where((source_of == order[0]) | (receiver == order[0]) | (sizes[receiver] == 0), 0, jnp.maximum(slack, 0))
    shifted = jax.random.randint(jax.random.fold_in(own, 4), (amount // 2,), 0, 1 << 20) % (slack + 1)
    sizes = sizes.at[source_of].add(-shifted).at[receiver].add(shifted)
    labels = jnp.searchsorted(jnp.cumsum(sizes), jnp.arange(rows * top), side="right").astype(jnp.int32)
    table = labels.reshape(top, rows).T
    table = table[jax.random.permutation(jax.random.fold_in(own, 1), rows)]
    turn = jax.random.randint(jax.random.fold_in(own, 2), (rows, 1), 0, top)
    return jnp.take_along_axis(table, (jnp.arange(top)[None, :] + turn) % top, axis=1)


def shares(count, total, limit, lean, full):
    weights = [(1 << 20) // math.isqrt(grade ** lean) + 1 for grade in range(1, count + 1)]
    largest = limit if full else min(limit, max(-(-total // count), total * weights[0] // sum(weights)))
    least = 1 if total - largest >= count - 1 else 0
    given, rest = [largest] + [least] * (count - 1), total - largest - least * (count - 1)
    while rest > 0:
        free = [i for i in range(1, count) if given[i] < largest] or [i for i in range(1, count) if given[i] < limit]
        mass, budget = sum([weights[i] for i in free]), rest
        for i in free:
            extra = min(limit - given[i], max(1, budget * weights[i] // mass), rest)
            given[i] = given[i] + extra
            rest = rest - extra
    return np.array(given)


def noise(rng, shape, deviation, bound, split=(), held_as=jnp.bfloat16):
    factor_of = steps_of(rng, shape, split, -0.22, 0.18) if split else 1.0
    entries = jax.random.normal(rng, shape, jnp.float32) * deviation * factor_of
    return jnp.minimum(jnp.maximum(entries, -bound), bound).astype(held_as)


def setup_inputs(seed: int = 0) -> dict:
    streams_of = jax.random.split(jax.random.key(seed), 11)
    counts = jnp.clip(2.0 * jax.random.uniform(streams_of[0], (NDOC, NB, 128), jnp.float32) ** steps_of(streams_of[0], (NDOC, NB, 128), ((0, 32),), -0.2, 0.2), 0.0, 2.0).astype(jnp.bfloat16)
    doc_owner_keys = jax.random.split(jax.random.fold_in(streams_of[1], 1), NDOC // DOC_DEV)
    doc_owner_turns = jax.random.permutation(jax.random.fold_in(streams_of[1], 3), NDOC // DOC_DEV)
    doc_owner = jax.vmap(lambda own, number: assign_block(jax.random.fold_in(streams_of[1], 2), own, number, DOC_DEV, DEVICES, NB, CAP, 2))(doc_owner_keys, doc_owner_turns).reshape((NDOC, NB))
    doc_sub = touch_ends(jax.random.randint(streams_of[2], (NDOC, NB), 0, VOC_DEV // 128), jax.random.fold_in(streams_of[2], 1), 0, (VOC_DEV // 128) - 1).astype(jnp.int32)
    doc_len = touch_ends(jax.random.randint(streams_of[3], (NDOC,), 64 * NB, 256 * NB), jax.random.fold_in(streams_of[3], 1), 64 * NB, (256 * NB) - 1).astype(jnp.int32)
    first_weight = noise(streams_of[4], (VOCAB, H), (128 * NB) ** -0.5, 0.25, ((0, 32),))
    first_bias = noise(streams_of[5], (H,), 0.5, 3.0, (), jnp.float32)
    head_weight = noise(streams_of[6], (H, K), H ** -0.5, 0.125, ((0, 4), (1, 8)))
    head_bias = noise(streams_of[7], (K,), 1.0, 4.0, (), jnp.float32)
    factor = draw_factor(jax.random.fold_in(streams_of[10], 71), 0)
    noise_draw = noise(streams_of[9], (NDOC, K), 1.0, 5.0, ((0, 32),))
    return dict(counts=counts, doc_owner=doc_owner, doc_sub=doc_sub, doc_len=doc_len, first_weight=first_weight, first_bias=first_bias, head_weight=head_weight, head_bias=head_bias, factor=factor, noise_draw=noise_draw)


def reference(counts, doc_owner, doc_sub, doc_len, first_weight, first_bias, head_weight, head_bias, factor, noise_draw):
    per_owner = VOC_DEV // 128
    window = DEVICES * CAP
    owner_flat = doc_owner.reshape(-1).astype(jnp.int32)
    sub_flat = doc_sub.reshape(-1).astype(jnp.int32)
    doc_flat = jnp.repeat(jnp.arange(NDOC, dtype=jnp.int32), NB)
    flat_rows = counts.reshape(-1, 128)
    row_order = jnp.argsort(owner_flat, stable=True)
    sorted_owner = owner_flat[row_order]
    starts = jnp.searchsorted(sorted_owner, jnp.arange(DEVICES, dtype=jnp.int32), side="left").astype(jnp.int32)
    padded_rows = jnp.concatenate([flat_rows[row_order], jnp.zeros((window, 128), counts.dtype)], axis=0)
    padded_sub = jnp.concatenate([sub_flat[row_order], jnp.zeros((window,), jnp.int32)], axis=0)
    padded_doc = jnp.concatenate([doc_flat[row_order], jnp.full((window,), NDOC, jnp.int32)], axis=0)
    padded_owner = jnp.concatenate([sorted_owner, jnp.full((window,), -1, jnp.int32)], axis=0)
    weight_blocks = first_weight.reshape(DEVICES, VOC_DEV, H)

    def owner_step(summed, owner_index):
        row_begin = starts[owner_index]
        rows_here = lax.dynamic_slice_in_dim(padded_rows, row_begin, window, 0)
        sub_here = lax.dynamic_slice_in_dim(padded_sub, row_begin, window, 0)
        doc_here = lax.dynamic_slice_in_dim(padded_doc, row_begin, window, 0)
        owner_here = lax.dynamic_slice_in_dim(padded_owner, row_begin, window, 0)
        row_valid = owner_here == owner_index
        select = ((sub_here[:, None] == jnp.arange(per_owner, dtype=jnp.int32)[None, :]) & row_valid[:, None]).astype(jnp.bfloat16)
        spread = (select[:, :, None] * rows_here[:, None, :]).reshape(window, per_owner * 128)
        owner_terms = jnp.dot(spread, weight_blocks[owner_index], preferred_element_type=jnp.float32).astype(jnp.bfloat16)
        doc_target = jnp.where(row_valid, doc_here, NDOC)
        summed = summed.at[doc_target].add(owner_terms.astype(jnp.float32), mode="drop")
        return summed, owner_index

    summed = lax.scan(owner_step, jnp.zeros((NDOC, H), jnp.float32), jnp.arange(DEVICES, dtype=jnp.int32))[0]
    length_scale = (128.0 * NB) / doc_len.astype(jnp.float32)
    hidden = jax.nn.softplus(summed * length_scale[:, None] + first_bias).astype(jnp.bfloat16)
    location = jnp.dot(hidden, head_weight, preferred_element_type=jnp.float32) + head_bias
    correlated = lax.dot_general(noise_draw, factor, (((1,), (1,)), ((), ())), preferred_element_type=jnp.float32)
    return (location + correlated).astype(jnp.bfloat16)
```

```python
import functools

import jax
import jax.numpy as jnp
from jax import lax
from jax.experimental import pallas as pl
from jax.experimental.pallas import tpu as pltpu
from jax.sharding import PartitionSpec as P

MESH = pl.DeviceIdType.MESH
F32 = jnp.float32
BF16 = jnp.bfloat16
CHIPS = (1, 4, 5)
CORE = 2
ORDER = (5, 7, 1, 3, 4, 6, 2)


def nt(a, b):
    return lax.dot_general(a, b, (((1,), (1,)), ((), ())), preferred_element_type=F32)


def tn(a, b):
    return lax.dot_general(a, b, (((0,), (0,)), ((), ())), preferred_element_type=F32)


def nn(a, b):
    return jnp.dot(a, b, preferred_element_type=F32)


def kernel(
    cap,
    counts_ref, owner_ref, sub_ref, scale_ref, weight_ref, bias_ref,
    head_ref, head_bias_ref, factor_ref, noise_ref,
    out_ref,
    cbuf, dtbuf, zin, dtin, pin, pmeta, spread, obuf, rbuf, zs, zr, own, dtp,
    head_all, fac_all, total,
    zc_s, zc_r, zd_s, zd_r, zw_s, zw_r, pc_s, pc_r, pm_s, pm_r,
    ret_s, ret_r, zp_s, zp_r, wp_s, wp_r, wc_s, wc_r,
):
    slots, docs, width = counts_ref.shape
    owners = 32
    rows = 8 * cap
    hc = head_ref.shape[1]
    v = lax.axis_index("vocab")
    d = lax.axis_index("docs")
    z = d // 2
    x = d % 2
    me = v * 2 + x

    def zpeer(k):
        return (v, (z ^ k) * 2 + x)

    def ppeer(r):
        j = me ^ r
        return (j // 2, z * 2 + j % 2)

    def rc(src, dst, s, r, dev):
        return pltpu.make_async_remote_copy(
            src_ref=src, dst_ref=dst, send_sem=s, recv_sem=r, device_id=dev, device_id_type=MESH
        )

    barrier = pltpu.get_barrier_semaphore()
    for k in range(1, 4):
        pl.semaphore_signal(barrier, inc=1, device_id=zpeer(k), device_id_type=MESH)
    for r in range(1, 8):
        pl.semaphore_signal(barrier, inc=1, device_id=ppeer(r), device_id_type=MESH)

    upper = jnp.where(
        lax.broadcasted_iota(jnp.int32, (docs, docs), 0)
        <= lax.broadcasted_iota(jnp.int32, (docs, docs), 1), 1.0, 0.0
    ).astype(BF16)
    owner_iota = lax.broadcasted_iota(jnp.int32, (owners, docs), 0)
    meta_iota = lax.broadcasted_iota(jnp.int32, (64, docs), 0)
    place_iota = lax.broadcasted_iota(jnp.int32, (128, docs), 0)
    row_iota = lax.broadcasted_iota(jnp.int32, (rows, docs), 0)
    carry = jnp.zeros((owners, 1), F32)
    meta = jnp.zeros((64, 128), F32)
    full = []
    for s in range(slots):
        o = owner_ref[s : s + 1, :]
        hot = jnp.where(owner_iota == o, 1.0, 0.0)
        cum = nn(hot.astype(BF16), upper) + carry
        carry = carry + jnp.sum(hot, axis=1, keepdims=True)
        pos = (jnp.sum(hot * cum, axis=0, keepdims=True) - 1.0).astype(jnp.int32)
        oz = (o >> 1) & 3
        oi = (o >> 3) * 2 + (o & 1)
        full.append(oz * rows + oi * cap + pos)
        named = jnp.where(
            meta_iota == oz * 16 + oi, jnp.broadcast_to(sub_ref[s : s + 1, :], (64, docs)).astype(F32), 0.0
        ).astype(BF16)
        placed = jnp.where(place_iota == pos, 1.0, 0.0).astype(BF16)
        meta = meta + nt(named, placed)
    for zo in range(4):
        acc = jnp.zeros((rows, width), F32)
        dt = jnp.zeros((rows, docs), F32)
        for s in range(slots):
            sel = jnp.where(row_iota + zo * rows == full[s], 1.0, 0.0)
            acc = acc + nn(sel.astype(BF16), counts_ref[s])
            dt = dt + sel
        cbuf[zo, 0:rows, :] = acc.astype(BF16)
        cbuf[zo, rows : rows + 16, :] = meta[zo * 16 : zo * 16 + 16, :].astype(BF16)
        dtbuf[zo] = dt.astype(BF16)

    pl.semaphore_wait(barrier, 10)

    def zc(k):
        return rc(cbuf.at[z ^ k], zin.at[k], zc_s.at[k], zc_r.at[k], zpeer(k))

    def zd(k):
        return rc(dtbuf.at[z ^ k], dtin.at[k], zd_s.at[k], zd_r.at[k], zpeer(k))

    def zw(k):
        return (
            rc(head_ref, head_all.at[v, z, x], zw_s.at[0, k], zw_r.at[0, k], zpeer(k)),
            rc(factor_ref, fac_all.at[v, z, x], zw_s.at[1, k], zw_r.at[1, k], zpeer(k)),
        )

    for k in (2, 3, 1):
        zc(k).start()
    for k in (2, 3, 1):
        zd(k).start()
        for c in zw(k):
            c.start()
    zin[0] = cbuf[z]
    dtin[0] = dtbuf[z]
    head_all[v, z, x] = head_ref[...]
    fac_all[v, z, x] = factor_ref[...]

    def pc(r):
        j = me ^ r
        return (
            rc(zin.at[:, pl.ds(pl.multiple_of(j * cap, cap), cap), :], pin.at[r], pc_s.at[r], pc_r.at[r], ppeer(r)),
            rc(zin.at[:, pl.ds(rows, 16), :], pmeta.at[r], pm_s.at[r], pm_r.at[r], ppeer(r)),
        )

    for k in range(1, 4):
        zc(k).wait_recv()
    for r in ORDER:
        for c in pc(r):
            c.start()
    pin[0] = zin[:, pl.ds(pl.multiple_of(me * cap, cap), cap), :]
    pmeta[0] = zin[:, rows : rows + 16, :]

    ones = jnp.ones((128, 128), BF16)
    pick = lax.broadcasted_iota(jnp.int32, (16, 128), 0) == me
    eye = lax.broadcasted_iota(jnp.int32, (cap, 128), 0) == lax.broadcasted_iota(jnp.int32, (cap, 128), 1)

    def spread_one(r, _):
        for k in range(4):
            line = jnp.sum(jnp.where(pick, pmeta[r, k].astype(F32), 0.0), axis=0, keepdims=True)
            sub = nn(jnp.where(eye, line, 0.0).astype(BF16), ones)
            got = pin[r, k].astype(F32)
            for b in range(8):
                spread[r, k * cap : (k + 1) * cap, b * width : (b + 1) * width] = jnp.where(
                    sub == float(b), got, 0.0
                ).astype(BF16)
        return 0

    spread_one(0, 0)
    for r in ORDER:
        for c in pc(r):
            c.wait_recv()
    lax.fori_loop(1, 8, spread_one, 0)

    def ret(h, r):
        return rc(
            obuf.at[h, r], rbuf.at[h, :, pl.ds(r * cap, cap), :], ret_s.at[h, r], ret_r.at[h, r], ppeer(r)
        )

    def owner_chunk(h, _):
        cols = weight_ref[:, pl.ds(pl.multiple_of(h * hc, hc), hc)]
        for pair in ((5, 7), (1, 3), (4, 6), (2, 0)):
            for r in pair:
                got = nn(spread[r], cols).astype(BF16).reshape(4, cap, hc)
                if r:
                    obuf[h, r] = got
                    ret(h, r).start()
                else:
                    rbuf[h, :, 0:cap, :] = got
        return 0

    lax.fori_loop(0, 4, owner_chunk, 0)

    def plane_copy(r):
        dev = ppeer(r)
        return (
            rc(head_all.at[v, :, x], head_all.at[v, :, x], wp_s.at[0, r], wp_r.at[0, r], dev),
            rc(fac_all.at[v, :, x], fac_all.at[v, :, x], wp_s.at[1, r], wp_r.at[1, r], dev),
        )

    def core_copy(r):
        dev = ppeer(CORE)
        j = me ^ r
        vv, xx = j // 2, j % 2
        return (
            rc(head_all.at[vv, :, xx], head_all.at[vv, :, xx], wc_s.at[0, r], wc_r.at[0, r], dev),
            rc(fac_all.at[vv, :, xx], fac_all.at[vv, :, xx], wc_s.at[1, r], wc_r.at[1, r], dev),
        )

    for k in range(1, 4):
        for c in zw(k):
            c.wait_recv()
    for r in CHIPS:
        for c in plane_copy(r):
            c.start()
    for c in core_copy(0):
        c.start()

    for k in range(1, 4):
        zd(k).wait_recv()
    for k in range(4):
        for r in range(8):
            dtp[k, r * cap : (r + 1) * cap, :] = dtin[k, pl.ds(pl.multiple_of((me ^ r) * cap, cap), cap), :]

    def zp(h, k):
        return rc(zs.at[h, k], zr.at[h, k], zp_s.at[h, k], zp_r.at[h, k], zpeer(k))

    def combine_chunk(h, _):
        for r in range(1, 8):
            ret(h, r).wait_recv()
        for k in (2, 3, 1):
            zs[h, k] = tn(dtp[k], rbuf[h, k]).astype(BF16)
            zp(h, k).start()
        own[h] = tn(dtp[0], rbuf[h, 0])
        return 0

    lax.fori_loop(0, 4, combine_chunk, 0)

    for r in CHIPS:
        for c in plane_copy(r):
            c.wait_recv()
        for c in core_copy(r):
            c.start()
    for r in (0,) + CHIPS:
        for c in core_copy(r):
            c.wait_recv()

    kc = factor_ref.shape[1]
    for w in range(4):
        block = fac_all[w].reshape(-1, kc)
        total[:, w * kc : (w + 1) * kc] = nn(noise_ref[...], block) + head_bias_ref[:, w * kc : (w + 1) * kc]

    def final_chunk(h, _):
        for k in range(1, 4):
            zp(h, k).wait_recv()
        summed = own[h]
        for k in range(1, 4):
            summed = summed + zr[h, k].astype(F32)
        value = summed * scale_ref[...] + bias_ref[h]
        hidden = (jnp.maximum(value, 0.0) + jnp.log1p(jnp.exp(-jnp.abs(value)))).astype(BF16)
        total[...] += nt(hidden, head_all[h].reshape(-1, hc))
        return 0

    lax.fori_loop(0, 4, final_chunk, 0)
    out_ref[...] = total[...].astype(BF16)

    for k in range(1, 4):
        zc(k).wait_send()
        zd(k).wait_send()
        for c in zw(k):
            c.wait_send()
    for r in range(1, 8):
        for c in pc(r):
            c.wait_send()
    for r in CHIPS:
        for c in plane_copy(r):
            c.wait_send()
    for r in (0,) + CHIPS:
        for c in core_copy(r):
            c.wait_send()

    def drain(h, _):
        for r in range(1, 8):
            ret(h, r).wait_send()
        for k in range(1, 4):
            zp(h, k).wait_send()
        return 0

    lax.fori_loop(0, 4, drain, 0)


def fused(
    counts, doc_owner, doc_sub, doc_len, first_weight, first_bias, head_weight, head_bias, factor, noise_draw
):
    docs, slots, width = counts.shape
    hidden = first_weight.shape[1]
    cap = 2 * docs * slots // 32
    hc, topics = head_weight.shape[0], head_bias.shape[0]
    rows = 8 * cap
    scale = (128.0 * slots / doc_len.astype(F32)).reshape(docs, 1)
    dma = pltpu.SemaphoreType.DMA
    kd, kc = head_weight.shape[1], factor.shape[0]
    return pl.pallas_call(
        functools.partial(kernel, cap),
        out_shape=jax.ShapeDtypeStruct((docs, topics), BF16),
        in_specs=[pl.BlockSpec(memory_space=pltpu.VMEM)] * 10,
        out_specs=pl.BlockSpec(memory_space=pltpu.VMEM),
        scratch_shapes=[
            pltpu.VMEM((4, rows + 16, width), BF16),
            pltpu.VMEM((4, rows, docs), BF16),
            pltpu.VMEM((4, rows + 16, width), BF16),
            pltpu.VMEM((4, rows, docs), BF16),
            pltpu.VMEM((8, 4, cap, width), BF16),
            pltpu.VMEM((8, 4, 16, 128), BF16),
            pltpu.VMEM((8, 4 * cap, 8 * width), BF16),
            pltpu.VMEM((4, 8, 4, cap, hc), BF16),
            pltpu.VMEM((4, 4, rows, hc), BF16),
            pltpu.VMEM((4, 4, docs, hc), BF16),
            pltpu.VMEM((4, 4, docs, hc), BF16),
            pltpu.VMEM((4, docs, hc), F32),
            pltpu.VMEM((4, rows, docs), BF16),
            pltpu.VMEM((4, 4, 2, kd, hc), BF16),
            pltpu.VMEM((4, 4, 2, factor.shape[1], kc), BF16),
            pltpu.VMEM((docs, topics), F32),
            dma((4,)), dma((4,)), dma((4,)), dma((4,)), dma((2, 4)), dma((2, 4)),
            dma((8,)), dma((8,)), dma((8,)), dma((8,)),
            dma((4, 8)), dma((4, 8)), dma((4, 4)), dma((4, 4)),
            dma((2, 8)), dma((2, 8)), dma((2, 8)), dma((2, 8)),
        ],
        compiler_params=pltpu.CompilerParams(
            collective_id=0, has_side_effects=True, vmem_limit_bytes=58 * 1024 * 1024
        ),
    )(
        jnp.transpose(counts, (1, 0, 2)),
        doc_owner.T,
        doc_sub.T,
        scale,
        first_weight,
        first_bias.reshape(4, 1, hc),
        head_weight.T,
        head_bias.reshape(1, -1),
        factor.T,
        noise_draw,
    )


def local(
    counts,
    doc_owner,
    doc_sub,
    doc_len,
    first_weight,
    first_bias,
    head_weight,
    head_bias,
    factor,
    noise_draw,
):
    vocab_devices = lax.axis_size("vocab")
    docs_devices = lax.axis_size("docs")
    device_count = vocab_devices * docs_devices
    docs_here, slot_count, block_width = counts.shape
    hidden_width = first_weight.shape[1]
    per_owner = first_weight.shape[0] // block_width
    capacity = max(2, 2 * docs_here * slot_count // device_count)
    owner_flat = doc_owner.reshape(-1)
    onehot = (owner_flat[:, None] == jnp.arange(device_count, dtype=jnp.int32)[None, :]).astype(
        jnp.int32
    )
    position = jnp.sum(jnp.cumsum(onehot, axis=0) * onehot, axis=1) - 1
    slot_index = owner_flat * capacity + position
    flat_rows = counts.reshape(-1, block_width)
    send_rows = (
        jnp.zeros((device_count * capacity, block_width), counts.dtype)
        .at[slot_index]
        .set(flat_rows)
    )
    send_sub = (
        jnp.zeros((device_count * capacity,), jnp.bfloat16)
        .at[slot_index]
        .set(doc_sub.reshape(-1).astype(jnp.bfloat16))
    )
    send_rows = send_rows.reshape(vocab_devices, docs_devices, capacity, block_width)
    send_sub = send_sub.reshape(vocab_devices, docs_devices, capacity)
    got_rows, got_sub = (
        lax.all_to_all(
            lax.all_to_all(send_rows, "vocab", split_axis=0, concat_axis=0, tiled=True),
            "docs",
            split_axis=1,
            concat_axis=1,
            tiled=True,
        ),
        lax.all_to_all(
            lax.all_to_all(send_sub, "vocab", split_axis=0, concat_axis=0, tiled=True),
            "docs",
            split_axis=1,
            concat_axis=1,
            tiled=True,
        ),
    )
    got_rows = got_rows.reshape(-1, block_width)
    got_sub = got_sub.reshape(-1).astype(jnp.int32)
    select = (got_sub[:, None] == jnp.arange(per_owner, dtype=jnp.int32)[None, :]).astype(
        jnp.bfloat16
    )
    spread = (select[:, :, None] * got_rows[:, None, :]).reshape(-1, per_owner * block_width)
    owner_terms = jnp.dot(spread, first_weight, preferred_element_type=jnp.float32).astype(
        jnp.bfloat16
    )
    owner_terms = owner_terms.reshape(vocab_devices, docs_devices, capacity, hidden_width)
    returned = lax.all_to_all(
        lax.all_to_all(owner_terms, "vocab", split_axis=0, concat_axis=0, tiled=True),
        "docs",
        split_axis=1,
        concat_axis=1,
        tiled=True,
    )
    returned = returned.reshape(-1, hidden_width)
    own_rows = returned[slot_index].reshape(docs_here, slot_count, hidden_width).astype(jnp.float32)
    summed = jnp.sum(own_rows, axis=1)
    length_scale = 128.0 * slot_count / doc_len.astype(jnp.float32)
    hidden = jax.nn.softplus(summed * length_scale[:, None] + first_bias).astype(jnp.bfloat16)
    panel_rows = lax.all_gather(head_weight, "docs", axis=1, tiled=True)
    location = jnp.dot(
        hidden,
        lax.all_gather(panel_rows, "vocab", axis=0, tiled=True),
        preferred_element_type=jnp.float32,
    )
    factor_panel = lax.all_gather(factor, "docs", axis=1, tiled=True)
    correlated = lax.dot_general(
        noise_draw,
        lax.all_gather(factor_panel, "vocab", axis=0, tiled=True),
        (((1,), (1,)), ((), ())),
        preferred_element_type=jnp.float32,
    )
    return (location + head_bias + correlated).astype(jnp.bfloat16)


def solution(mesh):
    small = mesh.shape["vocab"] == 4 and mesh.shape["docs"] == 8
    return jax.shard_map(
        fused if small else local,
        mesh=mesh,
        in_specs=(
            P(("vocab", "docs"), None, None),
            P(("vocab", "docs"), None),
            P(("vocab", "docs"), None),
            P(("vocab", "docs")),
            P(("vocab", "docs"), None),
            P(),
            P("vocab", "docs"),
            P(),
            P("vocab", "docs"),
            P(("vocab", "docs"), None),
        ),
        out_specs=P(("vocab", "docs"), None),
        check_vma=False,
    )
```

```python
import functools

import jax
import jax.numpy as jnp
from jax import lax
from jax.experimental import pallas as pl
from jax.experimental.pallas import tpu as pltpu
from jax.sharding import PartitionSpec as P

MESH = pl.DeviceIdType.MESH
F32 = jnp.float32
BF16 = jnp.bfloat16
X, Y, CORE = 1, 4, 2
ORDER = (5, 7, 1, 3, 4, 6, 2)


def nt(a, b):
    return lax.dot_general(a, b, (((1,), (1,)), ((), ())), preferred_element_type=F32)


def tn(a, b):
    return lax.dot_general(a, b, (((0,), (0,)), ((), ())), preferred_element_type=F32)


def nn(a, b):
    return jnp.dot(a, b, preferred_element_type=F32)


def kernel(
    cap,
    counts_ref, owner_ref, sub_ref, length_ref, weight_ref, bias_ref,
    head_ref, head_bias_ref, factor_ref, noise_ref,
    out_ref,
    cbuf, dtbuf, zin, dtin, pin, pmeta, spread, obuf, rbuf, zs, zr, own, dtp,
    head_all, fac_all, total, wide,
    zc_s, zc_r, zd_s, zd_r, zw_s, zw_r, pc_s, pc_r, pm_s, pm_r,
    ret_s, ret_r, zp_s, zp_r, wp_s, wp_r,
):
    slots, docs = owner_ref.shape
    width = counts_ref.shape[1]
    owners = 32
    rows = 8 * cap
    hc = head_ref.shape[1]
    v = lax.axis_index("vocab")
    d = lax.axis_index("docs")
    z = d // 2
    x = d % 2
    me = v * 2 + x

    def zpeer(k):
        return (v, (z ^ k) * 2 + x)

    def ppeer(r):
        j = me ^ r
        return (j // 2, z * 2 + j % 2)

    def rc(src, dst, s, r, dev):
        return pltpu.make_async_remote_copy(
            src_ref=src, dst_ref=dst, send_sem=s, recv_sem=r, device_id=dev, device_id_type=MESH
        )

    barrier = pltpu.get_barrier_semaphore()
    for k in range(1, 4):
        pl.semaphore_signal(barrier, inc=1, device_id=zpeer(k), device_id_type=MESH)
    for r in range(1, 8):
        pl.semaphore_signal(barrier, inc=1, device_id=ppeer(r), device_id_type=MESH)

    upper = jnp.where(
        lax.broadcasted_iota(jnp.int32, (docs, docs), 0)
        <= lax.broadcasted_iota(jnp.int32, (docs, docs), 1), 1.0, 0.0
    ).astype(BF16)
    owner_iota = lax.broadcasted_iota(jnp.int32, (owners, docs), 0)
    meta_iota = lax.broadcasted_iota(jnp.int32, (64, docs), 0)
    place_iota = lax.broadcasted_iota(jnp.int32, (128, docs), 0)
    row_iota = lax.broadcasted_iota(jnp.int32, (rows, docs), 0)
    carry = jnp.zeros((owners, 1), F32)
    wide[...] = counts_ref[...].astype(F32)
    counts = [wide[pl.ds(s, docs, stride=slots), :].astype(BF16) for s in range(slots)]
    meta = jnp.zeros((64, 128), F32)
    full = []
    for s in range(slots):
        o = owner_ref[s : s + 1, :]
        hot = jnp.where(owner_iota == o, 1.0, 0.0)
        cum = nn(hot.astype(BF16), upper) + carry
        carry = carry + jnp.sum(hot, axis=1, keepdims=True)
        pos = (jnp.sum(hot * cum, axis=0, keepdims=True) - 1.0).astype(jnp.int32)
        oz = (o >> 1) & 3
        oi = (o >> 3) * 2 + (o & 1)
        full.append(oz * rows + oi * cap + pos)
        named = jnp.where(
            meta_iota == oz * 16 + oi, jnp.broadcast_to(sub_ref[s : s + 1, :], (64, docs)).astype(F32), 0.0
        ).astype(BF16)
        placed = jnp.where(place_iota == pos, 1.0, 0.0).astype(BF16)
        meta = meta + nt(named, placed)
    for zo in range(4):
        acc = jnp.zeros((rows, width), F32)
        dt = jnp.zeros((rows, docs), F32)
        for s in range(slots):
            sel = jnp.where(row_iota + zo * rows == full[s], 1.0, 0.0)
            acc = acc + nn(sel.astype(BF16), counts[s])
            dt = dt + sel
        cbuf[zo, 0:rows, :] = acc.astype(BF16)
        cbuf[zo, rows : rows + 16, :] = meta[zo * 16 : zo * 16 + 16, :].astype(BF16)
        dtbuf[zo] = dt.astype(BF16)

    pl.semaphore_wait(barrier, 10)

    def zc(k):
        return rc(cbuf.at[z ^ k], zin.at[k], zc_s.at[k], zc_r.at[k], zpeer(k))

    def zd(k):
        return rc(dtbuf.at[z ^ k], dtin.at[k], zd_s.at[k], zd_r.at[k], zpeer(k))

    def zw(k):
        return (
            rc(head_ref, head_all.at[v, z, x], zw_s.at[0, k], zw_r.at[0, k], zpeer(k)),
            rc(factor_ref, fac_all.at[v, z, x], zw_s.at[1, k], zw_r.at[1, k], zpeer(k)),
        )

    def piece(t, k, r, hop):
        j = me ^ r
        ref = (head_all, fac_all)[t].at[j // 2, z ^ k, j % 2]
        rel = r ^ hop
        return rc(ref, ref, wp_s.at[t, k, rel], wp_r.at[t, k, rel], ppeer(hop))

    head_all[v, z, x] = head_ref[...]
    fac_all[v, z, x] = factor_ref[...]
    for k in (2, 3, 1):
        zc(k).start()
    for k in (2, 3, 1):
        for c in zw(k):
            c.start()
    for k in (2, 3, 1):
        zd(k).start()
    zin[0] = cbuf[z]
    dtin[0] = dtbuf[z]

    def pc(r):
        j = me ^ r
        return (
            rc(zin.at[:, pl.ds(pl.multiple_of(j * cap, cap), cap), :], pin.at[r], pc_s.at[r], pc_r.at[r], ppeer(r)),
            rc(zin.at[:, pl.ds(rows, 16), :], pmeta.at[r], pm_s.at[r], pm_r.at[r], ppeer(r)),
        )

    for k in range(1, 4):
        zc(k).wait_recv()
    for r in ORDER:
        for c in pc(r):
            c.start()
    for t in range(2):
        for hop in (X, Y, CORE):
            piece(t, 0, 0, hop).start()
    pin[0] = zin[:, pl.ds(pl.multiple_of(me * cap, cap), cap), :]
    pmeta[0] = zin[:, rows : rows + 16, :]

    ones = jnp.ones((128, 128), BF16)
    pick = lax.broadcasted_iota(jnp.int32, (16, 128), 0) == me
    eye = lax.broadcasted_iota(jnp.int32, (cap, 128), 0) == lax.broadcasted_iota(jnp.int32, (cap, 128), 1)

    def spread_one(r, _):
        for k in range(4):
            line = jnp.sum(jnp.where(pick, pmeta[r, k].astype(F32), 0.0), axis=0, keepdims=True)
            sub = nn(jnp.where(eye, line, 0.0).astype(BF16), ones)
            got = pin[r, k].astype(F32)
            for b in range(8):
                spread[r, k * cap : (k + 1) * cap, b * width : (b + 1) * width] = jnp.where(
                    sub == float(b), got, 0.0
                ).astype(BF16)
        return 0

    spread_one(0, 0)
    for r in ORDER:
        for c in pc(r):
            c.wait_recv()
    lax.fori_loop(1, 8, spread_one, 0)

    def ret(h, r):
        return rc(
            obuf.at[h, r], rbuf.at[h, :, pl.ds(r * cap, cap), :], ret_s.at[h, r], ret_r.at[h, r], ppeer(r)
        )

    def owner_chunk(h, _):
        cols = weight_ref[:, pl.ds(pl.multiple_of(h * hc, hc), hc)]
        for pair in ((5, 7), (1, 3), (4, 6), (2, 0)):
            for r in pair:
                got = nn(spread[r], cols).astype(BF16).reshape(4, cap, hc)
                if r:
                    obuf[h, r] = got
                    ret(h, r).start()
                else:
                    rbuf[h, :, 0:cap, :] = got
        return 0

    lax.fori_loop(0, 4, owner_chunk, 0)

    for k in range(1, 4):
        for t, c in enumerate(zw(k)):
            c.wait_recv()
            for hop in (X, Y, CORE):
                piece(t, k, 0, hop).start()

    def second(k):
        for t in range(2):
            first, then = ((X, Y), (Y, X))[t]
            piece(t, k, 0, first).wait_recv()
            piece(t, k, first, then).start()
            piece(t, k, first, CORE).start()
            piece(t, k, 0, then).wait_recv()
            piece(t, k, then, CORE).start()

    def third(k):
        for t in range(2):
            piece(t, k, X, Y).wait_recv()
            piece(t, k, X ^ Y, CORE).start()

    for k in range(1, 4):
        zd(k).wait_recv()
    for k in range(4):
        for r in range(8):
            dtp[k, r * cap : (r + 1) * cap, :] = dtin[k, pl.ds(pl.multiple_of((me ^ r) * cap, cap), cap), :]

    def zp(h, k):
        return rc(zs.at[h, k], zr.at[h, k], zp_s.at[h, k], zp_r.at[h, k], zpeer(k))

    def combine_chunk(h):
        for r in range(1, 8):
            ret(h, r).wait_recv()
        for k in (2, 3, 1):
            zs[h, k] = tn(dtp[k], rbuf[h, k]).astype(BF16)
            zp(h, k).start()
        own[h] = tn(dtp[0], rbuf[h, 0])

    second(0)
    for h in range(4):
        combine_chunk(h)
        third(h)
        if h < 3:
            second(h + 1)

    for k in range(4):
        for t in range(2):
            for r in (0, X, Y, X ^ Y):
                piece(t, k, r, CORE).wait_recv()

    docs_eye = lax.broadcasted_iota(jnp.int32, (docs, docs), 0) == lax.broadcasted_iota(jnp.int32, (docs, docs), 1)
    length = jnp.sum(jnp.where(docs_eye, length_ref[...].astype(F32), 0.0), axis=1, keepdims=True)
    scale = float(128 * slots) / length
    kc = factor_ref.shape[1]
    for w in range(4):
        block = fac_all[w].reshape(-1, kc)
        total[:, w * kc : (w + 1) * kc] = nn(noise_ref[...], block) + head_bias_ref[:, w * kc : (w + 1) * kc]

    def final_chunk(h, _):
        for k in range(1, 4):
            zp(h, k).wait_recv()
        summed = own[h]
        for k in range(1, 4):
            summed = summed + zr[h, k].astype(F32)
        value = summed * scale + bias_ref[h]
        hidden = (jnp.maximum(value, 0.0) + jnp.log1p(jnp.exp(-jnp.abs(value)))).astype(BF16)
        total[...] += nt(hidden, head_all[h].reshape(-1, hc))
        return 0

    lax.fori_loop(0, 4, final_chunk, 0)
    out_ref[...] = total[...].astype(BF16)

    for k in range(1, 4):
        zc(k).wait_send()
        zd(k).wait_send()
        for c in zw(k):
            c.wait_send()
    for r in range(1, 8):
        for c in pc(r):
            c.wait_send()
    for k in range(4):
        for t in range(2):
            first, then = ((X, Y), (Y, X))[t]
            piece(t, k, 0, X).wait_send()
            piece(t, k, 0, Y).wait_send()
            piece(t, k, first, then).wait_send()
            for r in (0, X, Y, X ^ Y):
                piece(t, k, r, CORE).wait_send()

    def drain(h, _):
        for r in range(1, 8):
            ret(h, r).wait_send()
        for k in range(1, 4):
            zp(h, k).wait_send()
        return 0

    lax.fori_loop(0, 4, drain, 0)


def fused(
    counts, doc_owner, doc_sub, doc_len, first_weight, first_bias, head_weight, head_bias, factor, noise_draw
):
    docs, slots, width = counts.shape
    hidden = first_weight.shape[1]
    cap = 2 * docs * slots // 32
    hc, topics = head_weight.shape[0], head_bias.shape[0]
    rows = 8 * cap
    dma = pltpu.SemaphoreType.DMA
    kd, kc = head_weight.shape[1], factor.shape[0]
    return pl.pallas_call(
        functools.partial(kernel, cap),
        out_shape=jax.ShapeDtypeStruct((docs, topics), BF16),
        in_specs=[pl.BlockSpec(memory_space=pltpu.VMEM)] * 10,
        out_specs=pl.BlockSpec(memory_space=pltpu.VMEM),
        scratch_shapes=[
            pltpu.VMEM((4, rows + 16, width), BF16),
            pltpu.VMEM((4, rows, docs), BF16),
            pltpu.VMEM((4, rows + 16, width), BF16),
            pltpu.VMEM((4, rows, docs), BF16),
            pltpu.VMEM((8, 4, cap, width), BF16),
            pltpu.VMEM((8, 4, 16, 128), BF16),
            pltpu.VMEM((8, 4 * cap, 8 * width), BF16),
            pltpu.VMEM((4, 8, 4, cap, hc), BF16),
            pltpu.VMEM((4, 4, rows, hc), BF16),
            pltpu.VMEM((4, 4, docs, hc), BF16),
            pltpu.VMEM((4, 4, docs, hc), BF16),
            pltpu.VMEM((4, docs, hc), F32),
            pltpu.VMEM((4, rows, docs), BF16),
            pltpu.VMEM((4, 4, 2, kd, hc), BF16),
            pltpu.VMEM((4, 4, 2, factor.shape[1], kc), BF16),
            pltpu.VMEM((docs, topics), F32),
            pltpu.VMEM((docs * slots, width), F32),
            dma((4,)), dma((4,)), dma((4,)), dma((4,)), dma((2, 4)), dma((2, 4)),
            dma((8,)), dma((8,)), dma((8,)), dma((8,)),
            dma((4, 8)), dma((4, 8)), dma((4, 4)), dma((4, 4)),
            dma((2, 4, 8)), dma((2, 4, 8)),
        ],
        compiler_params=pltpu.CompilerParams(
            collective_id=0, has_side_effects=True, vmem_limit_bytes=58 * 1024 * 1024
        ),
    )(
        counts.reshape(docs * slots, width),
        doc_owner.T,
        doc_sub.T,
        doc_len.reshape(1, docs),
        first_weight,
        first_bias.reshape(4, 1, hc),
        head_weight.T,
        head_bias.reshape(1, -1),
        factor.T,
        noise_draw,
    )


def local(
    counts,
    doc_owner,
    doc_sub,
    doc_len,
    first_weight,
    first_bias,
    head_weight,
    head_bias,
    factor,
    noise_draw,
):
    vocab_devices = lax.axis_size("vocab")
    docs_devices = lax.axis_size("docs")
    device_count = vocab_devices * docs_devices
    docs_here, slot_count, block_width = counts.shape
    hidden_width = first_weight.shape[1]
    per_owner = first_weight.shape[0] // block_width
    capacity = max(2, 2 * docs_here * slot_count // device_count)
    owner_flat = doc_owner.reshape(-1)
    onehot = (owner_flat[:, None] == jnp.arange(device_count, dtype=jnp.int32)[None, :]).astype(
        jnp.int32
    )
    position = jnp.sum(jnp.cumsum(onehot, axis=0) * onehot, axis=1) - 1
    slot_index = owner_flat * capacity + position
    flat_rows = counts.reshape(-1, block_width)
    send_rows = (
        jnp.zeros((device_count * capacity, block_width), counts.dtype)
        .at[slot_index]
        .set(flat_rows)
    )
    send_sub = (
        jnp.zeros((device_count * capacity,), jnp.bfloat16)
        .at[slot_index]
        .set(doc_sub.reshape(-1).astype(jnp.bfloat16))
    )
    send_rows = send_rows.reshape(vocab_devices, docs_devices, capacity, block_width)
    send_sub = send_sub.reshape(vocab_devices, docs_devices, capacity)
    got_rows, got_sub = (
        lax.all_to_all(
            lax.all_to_all(send_rows, "vocab", split_axis=0, concat_axis=0, tiled=True),
            "docs",
            split_axis=1,
            concat_axis=1,
            tiled=True,
        ),
        lax.all_to_all(
            lax.all_to_all(send_sub, "vocab", split_axis=0, concat_axis=0, tiled=True),
            "docs",
            split_axis=1,
            concat_axis=1,
            tiled=True,
        ),
    )
    got_rows = got_rows.reshape(-1, block_width)
    got_sub = got_sub.reshape(-1).astype(jnp.int32)
    select = (got_sub[:, None] == jnp.arange(per_owner, dtype=jnp.int32)[None, :]).astype(
        jnp.bfloat16
    )
    spread = (select[:, :, None] * got_rows[:, None, :]).reshape(-1, per_owner * block_width)
    owner_terms = jnp.dot(spread, first_weight, preferred_element_type=jnp.float32).astype(
        jnp.bfloat16
    )
    owner_terms = owner_terms.reshape(vocab_devices, docs_devices, capacity, hidden_width)
    returned = lax.all_to_all(
        lax.all_to_all(owner_terms, "vocab", split_axis=0, concat_axis=0, tiled=True),
        "docs",
        split_axis=1,
        concat_axis=1,
        tiled=True,
    )
    returned = returned.reshape(-1, hidden_width)
    own_rows = returned[slot_index].reshape(docs_here, slot_count, hidden_width).astype(jnp.float32)
    summed = jnp.sum(own_rows, axis=1)
    length_scale = 128.0 * slot_count / doc_len.astype(jnp.float32)
    hidden = jax.nn.softplus(summed * length_scale[:, None] + first_bias).astype(jnp.bfloat16)
    panel_rows = lax.all_gather(head_weight, "docs", axis=1, tiled=True)
    location = jnp.dot(
        hidden,
        lax.all_gather(panel_rows, "vocab", axis=0, tiled=True),
        preferred_element_type=jnp.float32,
    )
    factor_panel = lax.all_gather(factor, "docs", axis=1, tiled=True)
    correlated = lax.dot_general(
        noise_draw,
        lax.all_gather(factor_panel, "vocab", axis=0, tiled=True),
        (((1,), (1,)), ((), ())),
        preferred_element_type=jnp.float32,
    )
    return (location + head_bias + correlated).astype(jnp.bfloat16)


def solution(mesh):
    small = mesh.shape["vocab"] == 4 and mesh.shape["docs"] == 8
    return jax.shard_map(
        fused if small else local,
        mesh=mesh,
        in_specs=(
            P(("vocab", "docs"), None, None),
            P(("vocab", "docs"), None),
            P(("vocab", "docs"), None),
            P(("vocab", "docs")),
            P(("vocab", "docs"), None),
            P(),
            P("vocab", "docs"),
            P(),
            P("vocab", "docs"),
            P(("vocab", "docs"), None),
        ),
        out_specs=P(("vocab", "docs"), None),
        check_vma=False,
    )
```

```python
import functools

import jax
import jax.numpy as jnp
from jax import lax
from jax.experimental import pallas as pl
from jax.experimental.pallas import tpu as pltpu
from jax.sharding import PartitionSpec as P

MESH = pl.DeviceIdType.MESH
F32 = jnp.float32
BF16 = jnp.bfloat16
X, Y, CORE = 1, 4, 2
ORDER = (5, 7, 1, 3, 4, 6, 2)


def nt(a, b):
    return lax.dot_general(a, b, (((1,), (1,)), ((), ())), preferred_element_type=F32)


def tn(a, b):
    return lax.dot_general(a, b, (((0,), (0,)), ((), ())), preferred_element_type=F32)


def nn(a, b):
    return jnp.dot(a, b, preferred_element_type=F32)


def kernel(
    cap,
    counts_ref, owner_ref, sub_ref, length_ref, weight_ref, bias_ref,
    head_ref, factor_ref, noise_ref,
    total,
    cbuf, dtbuf, zin, dtin, pin, pmeta, spread, obuf, rbuf, zs, zr, own, dtp,
    head_all, fac_all, wide,
    zc_s, zc_r, zd_s, zd_r, zw_s, zw_r, pc_s, pc_r, pm_s, pm_r,
    ret_s, ret_r, zp_s, zp_r, wp_s, wp_r,
):
    slots, docs = owner_ref.shape
    width = counts_ref.shape[1]
    owners = 32
    rows = 8 * cap
    hc = head_ref.shape[1]
    v = lax.axis_index("vocab")
    d = lax.axis_index("docs")
    z = d // 2
    x = d % 2
    me = v * 2 + x

    def zpeer(k):
        return (v, (z ^ k) * 2 + x)

    def ppeer(r):
        j = me ^ r
        return (j // 2, z * 2 + j % 2)

    def rc(src, dst, s, r, dev):
        return pltpu.make_async_remote_copy(
            src_ref=src, dst_ref=dst, send_sem=s, recv_sem=r, device_id=dev, device_id_type=MESH
        )

    barrier = pltpu.get_barrier_semaphore()
    for k in range(1, 4):
        pl.semaphore_signal(barrier, inc=1, device_id=zpeer(k), device_id_type=MESH)
    for r in range(1, 8):
        pl.semaphore_signal(barrier, inc=1, device_id=ppeer(r), device_id_type=MESH)

    upper = jnp.where(
        lax.broadcasted_iota(jnp.int32, (docs, docs), 0)
        <= lax.broadcasted_iota(jnp.int32, (docs, docs), 1), 1.0, 0.0
    ).astype(BF16)
    owner_iota = lax.broadcasted_iota(jnp.int32, (owners, docs), 0)
    meta_iota = lax.broadcasted_iota(jnp.int32, (64, docs), 0)
    place_iota = lax.broadcasted_iota(jnp.int32, (128, docs), 0)
    row_iota = lax.broadcasted_iota(jnp.int32, (rows, docs), 0)
    carry = jnp.zeros((owners, 1), F32)
    wide[...] = counts_ref[...].astype(F32)
    counts = [wide[pl.ds(s, docs, stride=slots), :].astype(BF16) for s in range(slots)]
    meta = jnp.zeros((64, 128), F32)
    full = []
    for s in range(slots):
        o = owner_ref[s : s + 1, :]
        hot = jnp.where(owner_iota == o, 1.0, 0.0)
        cum = nn(hot.astype(BF16), upper) + carry
        carry = carry + jnp.sum(hot, axis=1, keepdims=True)
        pos = (jnp.sum(hot * cum, axis=0, keepdims=True) - 1.0).astype(jnp.int32)
        oz = (o >> 1) & 3
        oi = (o >> 3) * 2 + (o & 1)
        full.append(oz * rows + oi * cap + pos)
        named = jnp.where(
            meta_iota == oz * 16 + oi, jnp.broadcast_to(sub_ref[s : s + 1, :], (64, docs)).astype(F32), 0.0
        ).astype(BF16)
        placed = jnp.where(place_iota == pos, 1.0, 0.0).astype(BF16)
        meta = meta + nt(named, placed)
    for zo in range(4):
        acc = jnp.zeros((rows, width), F32)
        dt = jnp.zeros((rows, docs), F32)
        for s in range(slots):
            sel = jnp.where(row_iota + zo * rows == full[s], 1.0, 0.0)
            acc = acc + nn(sel.astype(BF16), counts[s])
            dt = dt + sel
        cbuf[zo, 0:rows, :] = acc.astype(BF16)
        cbuf[zo, rows : rows + 16, :] = meta[zo * 16 : zo * 16 + 16, :].astype(BF16)
        dtbuf[zo] = dt.astype(BF16)

    pl.semaphore_wait(barrier, 10)

    def zc(k):
        return rc(cbuf.at[z ^ k], zin.at[k], zc_s.at[k], zc_r.at[k], zpeer(k))

    def zd(k):
        return rc(dtbuf.at[z ^ k], dtin.at[k], zd_s.at[k], zd_r.at[k], zpeer(k))

    def zw(k):
        return (
            rc(head_ref, head_all.at[v, z, x], zw_s.at[0, k], zw_r.at[0, k], zpeer(k)),
            rc(factor_ref, fac_all.at[v, z, x], zw_s.at[1, k], zw_r.at[1, k], zpeer(k)),
        )

    def piece(t, k, r, hop):
        j = me ^ r
        ref = (head_all, fac_all)[t].at[j // 2, z ^ k, j % 2]
        rel = r ^ hop
        return rc(ref, ref, wp_s.at[t, k, rel], wp_r.at[t, k, rel], ppeer(hop))

    head_all[v, z, x] = head_ref[...]
    fac_all[v, z, x] = factor_ref[...]
    for k in (2, 3, 1):
        zc(k).start()
    zin[0] = cbuf[z]
    dtin[0] = dtbuf[z]

    def pc(r):
        j = me ^ r
        return (
            rc(zin.at[:, pl.ds(pl.multiple_of(j * cap, cap), cap), :], pin.at[r], pc_s.at[r], pc_r.at[r], ppeer(r)),
            rc(zin.at[:, pl.ds(rows, 16), :], pmeta.at[r], pm_s.at[r], pm_r.at[r], ppeer(r)),
        )

    for k in range(1, 4):
        zc(k).wait_recv()
    for r in ORDER:
        for c in pc(r):
            c.start()
    for k in (2, 3, 1):
        for c in zw(k):
            c.start()
    for k in (2, 3, 1):
        zd(k).start()
    for t in range(2):
        for hop in (X, Y, CORE):
            piece(t, 0, 0, hop).start()
    pin[0] = zin[:, pl.ds(pl.multiple_of(me * cap, cap), cap), :]
    pmeta[0] = zin[:, rows : rows + 16, :]

    ones = jnp.ones((128, 128), BF16)
    pick = lax.broadcasted_iota(jnp.int32, (16, 128), 0) == me
    eye = lax.broadcasted_iota(jnp.int32, (cap, 128), 0) == lax.broadcasted_iota(jnp.int32, (cap, 128), 1)

    def spread_one(r, _):
        for k in range(4):
            line = jnp.sum(jnp.where(pick, pmeta[r, k].astype(F32), 0.0), axis=0, keepdims=True)
            sub = nn(jnp.where(eye, line, 0.0).astype(BF16), ones)
            got = pin[r, k].astype(F32)
            for b in range(8):
                spread[r, k * cap : (k + 1) * cap, b * width : (b + 1) * width] = jnp.where(
                    sub == float(b), got, 0.0
                ).astype(BF16)
        return 0

    spread_one(0, 0)
    for r in ORDER:
        for c in pc(r):
            c.wait_recv()
    lax.fori_loop(1, 8, spread_one, 0)

    def ret(h, r):
        return rc(
            obuf.at[h, r], rbuf.at[h, :, pl.ds(r * cap, cap), :], ret_s.at[h, r], ret_r.at[h, r], ppeer(r)
        )

    def owner_chunk(h, _):
        cols = weight_ref[:, pl.ds(pl.multiple_of(h * hc, hc), hc)]
        for pair in ((5, 7), (1, 3), (4, 6), (2, 0)):
            for r in pair:
                got = nn(spread[r], cols).astype(BF16).reshape(4, cap, hc)
                if r:
                    obuf[h, r] = got
                    ret(h, r).start()
                else:
                    rbuf[h, :, 0:cap, :] = got
        return 0

    lax.fori_loop(0, 4, owner_chunk, 0)

    for k in range(1, 4):
        for t, c in enumerate(zw(k)):
            c.wait_recv()
            for hop in (X, Y, CORE):
                piece(t, k, 0, hop).start()

    def second(k):
        for t in range(2):
            first, then = ((X, Y), (Y, X))[t]
            piece(t, k, 0, first).wait_recv()
            piece(t, k, first, then).start()
            piece(t, k, first, CORE).start()
            piece(t, k, 0, then).wait_recv()
            piece(t, k, then, CORE).start()

    def third(k):
        for t in range(2):
            piece(t, k, X, Y).wait_recv()
            piece(t, k, X ^ Y, CORE).start()

    for k in range(1, 4):
        zd(k).wait_recv()
    for k in range(4):
        for r in range(8):
            dtp[k, r * cap : (r + 1) * cap, :] = dtin[k, pl.ds(pl.multiple_of((me ^ r) * cap, cap), cap), :]

    def zp(h, k):
        return rc(zs.at[h, k], zr.at[h, k], zp_s.at[h, k], zp_r.at[h, k], zpeer(k))

    def combine_chunk(h):
        for r in range(1, 8):
            ret(h, r).wait_recv()
        for k in (2, 3, 1):
            zs[h, k] = tn(dtp[k], rbuf[h, k]).astype(BF16)
            zp(h, k).start()
        own[h] = tn(dtp[0], rbuf[h, 0])

    second(0)
    for h in range(4):
        combine_chunk(h)
    for k in range(1, 4):
        second(k)
    for k in range(4):
        third(k)

    for k in range(4):
        for t in range(2):
            for r in (0, X, Y, X ^ Y):
                piece(t, k, r, CORE).wait_recv()

    docs_eye = lax.broadcasted_iota(jnp.int32, (docs, docs), 0) == lax.broadcasted_iota(jnp.int32, (docs, docs), 1)
    length = jnp.sum(jnp.where(docs_eye, length_ref[...].astype(F32), 0.0), axis=1, keepdims=True)
    scale = float(128 * slots) / length
    kc = factor_ref.shape[1]
    for w in range(4):
        block = fac_all[w].reshape(-1, kc)
        total[:, w * kc : (w + 1) * kc] = nn(noise_ref[...], block)

    def final_chunk(h, _):
        for k in range(1, 4):
            zp(h, k).wait_recv()
        summed = own[h]
        for k in range(1, 4):
            summed = summed + zr[h, k].astype(F32)
        value = summed * scale + bias_ref[h]
        hidden = (jnp.maximum(value, 0.0) + jnp.log1p(jnp.exp(-jnp.abs(value)))).astype(BF16)
        total[...] += nt(hidden, head_all[h].reshape(-1, hc))
        return 0

    lax.fori_loop(0, 4, final_chunk, 0)

    for k in range(1, 4):
        zc(k).wait_send()
        zd(k).wait_send()
        for c in zw(k):
            c.wait_send()
    for r in range(1, 8):
        for c in pc(r):
            c.wait_send()
    for k in range(4):
        for t in range(2):
            first, then = ((X, Y), (Y, X))[t]
            piece(t, k, 0, X).wait_send()
            piece(t, k, 0, Y).wait_send()
            piece(t, k, first, then).wait_send()
            for r in (0, X, Y, X ^ Y):
                piece(t, k, r, CORE).wait_send()

    def drain(h, _):
        for r in range(1, 8):
            ret(h, r).wait_send()
        for k in range(1, 4):
            zp(h, k).wait_send()
        return 0

    lax.fori_loop(0, 4, drain, 0)


def fused(
    counts, doc_owner, doc_sub, doc_len, first_weight, first_bias, head_weight, head_bias, factor, noise_draw
):
    docs, slots, width = counts.shape
    hidden = first_weight.shape[1]
    cap = 2 * docs * slots // 32
    hc, topics = head_weight.shape[0], head_bias.shape[0]
    rows = 8 * cap
    dma = pltpu.SemaphoreType.DMA
    kd, kc = head_weight.shape[1], factor.shape[0]
    total = pl.pallas_call(
        functools.partial(kernel, cap),
        out_shape=jax.ShapeDtypeStruct((docs, topics), F32),
        in_specs=[pl.BlockSpec(memory_space=pltpu.VMEM)] * 9,
        out_specs=pl.BlockSpec(memory_space=pltpu.VMEM),
        scratch_shapes=[
            pltpu.VMEM((4, rows + 16, width), BF16),
            pltpu.VMEM((4, rows, docs), BF16),
            pltpu.VMEM((4, rows + 16, width), BF16),
            pltpu.VMEM((4, rows, docs), BF16),
            pltpu.VMEM((8, 4, cap, width), BF16),
            pltpu.VMEM((8, 4, 16, 128), BF16),
            pltpu.VMEM((8, 4 * cap, 8 * width), BF16),
            pltpu.VMEM((4, 8, 4, cap, hc), BF16),
            pltpu.VMEM((4, 4, rows, hc), BF16),
            pltpu.VMEM((4, 4, docs, hc), BF16),
            pltpu.VMEM((4, 4, docs, hc), BF16),
            pltpu.VMEM((4, docs, hc), F32),
            pltpu.VMEM((4, rows, docs), BF16),
            pltpu.VMEM((4, 4, 2, kd, hc), BF16),
            pltpu.VMEM((4, 4, 2, factor.shape[1], kc), BF16),
            pltpu.VMEM((docs * slots, width), F32),
            dma((4,)), dma((4,)), dma((4,)), dma((4,)), dma((2, 4)), dma((2, 4)),
            dma((8,)), dma((8,)), dma((8,)), dma((8,)),
            dma((4, 8)), dma((4, 8)), dma((4, 4)), dma((4, 4)),
            dma((2, 4, 8)), dma((2, 4, 8)),
        ],
        compiler_params=pltpu.CompilerParams(
            collective_id=0, has_side_effects=True, vmem_limit_bytes=58 * 1024 * 1024
        ),
    )(
        counts.reshape(docs * slots, width),
        doc_owner.T,
        doc_sub.T,
        doc_len.reshape(1, docs),
        first_weight,
        first_bias.reshape(4, 1, hc),
        head_weight.T,
        factor.T,
        noise_draw,
    )
    return (total + head_bias).astype(BF16)


def local(
    counts,
    doc_owner,
    doc_sub,
    doc_len,
    first_weight,
    first_bias,
    head_weight,
    head_bias,
    factor,
    noise_draw,
):
    vocab_devices = lax.axis_size("vocab")
    docs_devices = lax.axis_size("docs")
    device_count = vocab_devices * docs_devices
    docs_here, slot_count, block_width = counts.shape
    hidden_width = first_weight.shape[1]
    per_owner = first_weight.shape[0] // block_width
    capacity = max(2, 2 * docs_here * slot_count // device_count)
    owner_flat = doc_owner.reshape(-1)
    onehot = (owner_flat[:, None] == jnp.arange(device_count, dtype=jnp.int32)[None, :]).astype(
        jnp.int32
    )
    position = jnp.sum(jnp.cumsum(onehot, axis=0) * onehot, axis=1) - 1
    slot_index = owner_flat * capacity + position
    flat_rows = counts.reshape(-1, block_width)
    send_rows = (
        jnp.zeros((device_count * capacity, block_width), counts.dtype)
        .at[slot_index]
        .set(flat_rows)
    )
    send_sub = (
        jnp.zeros((device_count * capacity,), jnp.bfloat16)
        .at[slot_index]
        .set(doc_sub.reshape(-1).astype(jnp.bfloat16))
    )
    send_rows = send_rows.reshape(vocab_devices, docs_devices, capacity, block_width)
    send_sub = send_sub.reshape(vocab_devices, docs_devices, capacity)
    got_rows, got_sub = (
        lax.all_to_all(
            lax.all_to_all(send_rows, "vocab", split_axis=0, concat_axis=0, tiled=True),
            "docs",
            split_axis=1,
            concat_axis=1,
            tiled=True,
        ),
        lax.all_to_all(
            lax.all_to_all(send_sub, "vocab", split_axis=0, concat_axis=0, tiled=True),
            "docs",
            split_axis=1,
            concat_axis=1,
            tiled=True,
        ),
    )
    got_rows = got_rows.reshape(-1, block_width)
    got_sub = got_sub.reshape(-1).astype(jnp.int32)
    select = (got_sub[:, None] == jnp.arange(per_owner, dtype=jnp.int32)[None, :]).astype(
        jnp.bfloat16
    )
    spread = (select[:, :, None] * got_rows[:, None, :]).reshape(-1, per_owner * block_width)
    owner_terms = jnp.dot(spread, first_weight, preferred_element_type=jnp.float32).astype(
        jnp.bfloat16
    )
    owner_terms = owner_terms.reshape(vocab_devices, docs_devices, capacity, hidden_width)
    returned = lax.all_to_all(
        lax.all_to_all(owner_terms, "vocab", split_axis=0, concat_axis=0, tiled=True),
        "docs",
        split_axis=1,
        concat_axis=1,
        tiled=True,
    )
    returned = returned.reshape(-1, hidden_width)
    own_rows = returned[slot_index].reshape(docs_here, slot_count, hidden_width).astype(jnp.float32)
    summed = jnp.sum(own_rows, axis=1)
    length_scale = 128.0 * slot_count / doc_len.astype(jnp.float32)
    hidden = jax.nn.softplus(summed * length_scale[:, None] + first_bias).astype(jnp.bfloat16)
    panel_rows = lax.all_gather(head_weight, "docs", axis=1, tiled=True)
    location = jnp.dot(
        hidden,
        lax.all_gather(panel_rows, "vocab", axis=0, tiled=True),
        preferred_element_type=jnp.float32,
    )
    factor_panel = lax.all_gather(factor, "docs", axis=1, tiled=True)
    correlated = lax.dot_general(
        noise_draw,
        lax.all_gather(factor_panel, "vocab", axis=0, tiled=True),
        (((1,), (1,)), ((), ())),
        preferred_element_type=jnp.float32,
    )
    return (location + head_bias + correlated).astype(jnp.bfloat16)


def solution(mesh):
    small = mesh.shape["vocab"] == 4 and mesh.shape["docs"] == 8
    return jax.shard_map(
        fused if small else local,
        mesh=mesh,
        in_specs=(
            P(("vocab", "docs"), None, None),
            P(("vocab", "docs"), None),
            P(("vocab", "docs"), None),
            P(("vocab", "docs")),
            P(("vocab", "docs"), None),
            P(),
            P("vocab", "docs"),
            P(),
            P("vocab", "docs"),
            P(("vocab", "docs"), None),
        ),
        out_specs=P(("vocab", "docs"), None),
        check_vma=False,
    )
```

```python
import functools

import jax
import jax.numpy as jnp
from jax import lax
from jax.experimental import pallas as pl
from jax.experimental.pallas import tpu as pltpu
from jax.sharding import PartitionSpec as P

MESH = pl.DeviceIdType.MESH
F32 = jnp.float32
BF16 = jnp.bfloat16
X, Y, CORE = 1, 4, 2
ORDER = (5, 7, 1, 3, 4, 6, 2)


def nt(a, b):
    return lax.dot_general(a, b, (((1,), (1,)), ((), ())), preferred_element_type=F32)


def tn(a, b):
    return lax.dot_general(a, b, (((0,), (0,)), ((), ())), preferred_element_type=F32)


def nn(a, b):
    return jnp.dot(a, b, preferred_element_type=F32)


def kernel(
    cap,
    counts_ref, owner_ref, sub_ref, length_ref, weight_ref, bias_ref,
    head_ref, factor_ref, noise_ref,
    total,
    cbuf, dtbuf, zin, dtin, pin, pmeta, spread, obuf, rbuf, zs, zr, own, dtp,
    head_all, fac_all, wide,
    zc_s, zc_r, zd_s, zd_r, zw_s, zw_r, pc_s, pc_r, pm_s, pm_r,
    ret_s, ret_r, zp_s, zp_r, wp_s, wp_r,
):
    slots, docs = owner_ref.shape
    width = counts_ref.shape[1]
    owners = 32
    rows = 8 * cap
    hc = head_ref.shape[1]
    v = lax.axis_index("vocab")
    d = lax.axis_index("docs")
    z = d // 2
    x = d % 2
    me = v * 2 + x

    def zpeer(k):
        return (v, (z ^ k) * 2 + x)

    def ppeer(r):
        j = me ^ r
        return (j // 2, z * 2 + j % 2)

    def rc(src, dst, s, r, dev):
        return pltpu.make_async_remote_copy(
            src_ref=src, dst_ref=dst, send_sem=s, recv_sem=r, device_id=dev, device_id_type=MESH
        )

    barrier = pltpu.get_barrier_semaphore()
    for k in range(1, 4):
        pl.semaphore_signal(barrier, inc=1, device_id=zpeer(k), device_id_type=MESH)
    for r in range(1, 8):
        pl.semaphore_signal(barrier, inc=1, device_id=ppeer(r), device_id_type=MESH)

    upper = jnp.where(
        lax.broadcasted_iota(jnp.int32, (docs, docs), 0)
        <= lax.broadcasted_iota(jnp.int32, (docs, docs), 1), 1.0, 0.0
    ).astype(BF16)
    owner_iota = lax.broadcasted_iota(jnp.int32, (owners, docs), 0)
    meta_iota = lax.broadcasted_iota(jnp.int32, (64, docs), 0)
    place_iota = lax.broadcasted_iota(jnp.int32, (128, docs), 0)
    row_iota = lax.broadcasted_iota(jnp.int32, (rows, docs), 0)
    carry = jnp.zeros((owners, 1), F32)
    wide[...] = counts_ref[...].astype(F32)
    counts = [wide[pl.ds(s, docs, stride=slots), :].astype(BF16) for s in range(slots)]
    meta = jnp.zeros((64, 128), F32)
    full = []
    for s in range(slots):
        o = owner_ref[s : s + 1, :]
        hot = jnp.where(owner_iota == o, 1.0, 0.0)
        cum = nn(hot.astype(BF16), upper) + carry
        carry = carry + jnp.sum(hot, axis=1, keepdims=True)
        pos = (jnp.sum(hot * cum, axis=0, keepdims=True) - 1.0).astype(jnp.int32)
        oz = (o >> 1) & 3
        oi = (o >> 3) * 2 + (o & 1)
        full.append(oz * rows + oi * cap + pos)
        named = jnp.where(
            meta_iota == oz * 16 + oi, jnp.broadcast_to(sub_ref[s : s + 1, :], (64, docs)).astype(F32), 0.0
        ).astype(BF16)
        placed = jnp.where(place_iota == pos, 1.0, 0.0).astype(BF16)
        meta = meta + nt(named, placed)
    for zo in range(4):
        acc = jnp.zeros((rows, width), F32)
        dt = jnp.zeros((rows, docs), F32)
        for s in range(slots):
            sel = jnp.where(row_iota + zo * rows == full[s], 1.0, 0.0)
            acc = acc + nn(sel.astype(BF16), counts[s])
            dt = dt + sel
        cbuf[zo, 0:rows, :] = acc.astype(BF16)
        cbuf[zo, rows : rows + 16, :] = meta[zo * 16 : zo * 16 + 16, :].astype(BF16)
        dtbuf[zo] = dt.astype(BF16)

    pl.semaphore_wait(barrier, 10)

    def zc(k):
        return rc(cbuf.at[z ^ k], zin.at[k], zc_s.at[k], zc_r.at[k], zpeer(k))

    def zd(k):
        return rc(dtbuf.at[z ^ k], dtin.at[k], zd_s.at[k], zd_r.at[k], zpeer(k))

    def zw(k):
        return (
            rc(head_ref, head_all.at[v, z, x], zw_s.at[0, k], zw_r.at[0, k], zpeer(k)),
            rc(factor_ref, fac_all.at[v, z, x], zw_s.at[1, k], zw_r.at[1, k], zpeer(k)),
        )

    def piece(t, k, r, hop):
        j = me ^ r
        ref = (head_all, fac_all)[t].at[j // 2, z ^ k, j % 2]
        rel = r ^ hop
        return rc(ref, ref, wp_s.at[t, k, rel], wp_r.at[t, k, rel], ppeer(hop or CORE))

    def guarded(t, held, act):
        if t:
            pl.when(held)(act)
        else:
            act()

    def go(t, k, r, hop):
        guarded(t, (z ^ k) <= (me ^ r) // 2, lambda: piece(t, k, r, hop).start())

    def sent(t, k, r, hop):
        guarded(t, (z ^ k) <= (me ^ r) // 2, lambda: piece(t, k, r, hop).wait_send())

    def got(t, k, rel):
        guarded(t, (z ^ k) <= (me ^ rel) // 2, lambda: piece(t, k, rel, 0).wait_recv())

    def turn(t, k):
        return (Y, X) if t or k == 3 else (X, Y)

    head_all[v, z, x] = head_ref[...]
    fac_all[v, z, x] = factor_ref[...]
    for k in (2, 3, 1):
        zc(k).start()
    zin[0] = cbuf[z]
    dtin[0] = dtbuf[z]

    def pc(r):
        j = me ^ r
        return (
            rc(zin.at[:, pl.ds(pl.multiple_of(j * cap, cap), cap), :], pin.at[r], pc_s.at[r], pc_r.at[r], ppeer(r)),
            rc(zin.at[:, pl.ds(rows, 16), :], pmeta.at[r], pm_s.at[r], pm_r.at[r], ppeer(r)),
        )

    for k in range(1, 4):
        zc(k).wait_recv()
    for r in ORDER:
        for c in pc(r):
            c.start()
    for k in (2, 3, 1):
        for t, c in enumerate(zw(k)):
            guarded(t, z <= v, c.start)
    for k in (2, 3, 1):
        zd(k).start()
    for t in range(2):
        for hop in (X, Y, CORE):
            go(t, 0, 0, hop)
    pin[0] = zin[:, pl.ds(pl.multiple_of(me * cap, cap), cap), :]
    pmeta[0] = zin[:, rows : rows + 16, :]

    ones = jnp.ones((128, 128), BF16)
    pick = lax.broadcasted_iota(jnp.int32, (16, 128), 0) == me
    eye = lax.broadcasted_iota(jnp.int32, (cap, 128), 0) == lax.broadcasted_iota(jnp.int32, (cap, 128), 1)

    def spread_one(r, _):
        for k in range(4):
            line = jnp.sum(jnp.where(pick, pmeta[r, k].astype(F32), 0.0), axis=0, keepdims=True)
            sub = nn(jnp.where(eye, line, 0.0).astype(BF16), ones)
            got = pin[r, k].astype(F32)
            for b in range(8):
                spread[r, k * cap : (k + 1) * cap, b * width : (b + 1) * width] = jnp.where(
                    sub == float(b), got, 0.0
                ).astype(BF16)
        return 0

    spread_one(0, 0)
    for r in ORDER:
        for c in pc(r):
            c.wait_recv()
    lax.fori_loop(1, 8, spread_one, 0)

    def ret(h, r):
        return rc(
            obuf.at[h, r], rbuf.at[h, :, pl.ds(r * cap, cap), :], ret_s.at[h, r], ret_r.at[h, r], ppeer(r)
        )

    def owner_chunk(h, _):
        cols = weight_ref[:, pl.ds(pl.multiple_of(h * hc, hc), hc)]
        for pair in ((5, 7), (1, 3), (4, 6), (2, 0)):
            for r in pair:
                got = nn(spread[r], cols).astype(BF16).reshape(4, cap, hc)
                if r:
                    obuf[h, r] = got
                    ret(h, r).start()
                else:
                    rbuf[h, :, 0:cap, :] = got
        return 0

    lax.fori_loop(0, 4, owner_chunk, 0)

    for k in range(1, 4):
        for t, c in enumerate(zw(k)):
            guarded(t, (z ^ k) <= v, c.wait_recv)
            for hop in (X, Y, CORE):
                go(t, k, 0, hop)

    def second(k):
        for t in range(2):
            first, then = turn(t, k)
            got(t, k, first)
            go(t, k, first, then)
            go(t, k, first, CORE)
            got(t, k, then)
            go(t, k, then, CORE)

    def third(k):
        for t in range(2):
            got(t, k, X ^ Y)
            go(t, k, X ^ Y, CORE)

    for k in range(1, 4):
        zd(k).wait_recv()
    for k in range(4):
        for r in range(8):
            dtp[k, r * cap : (r + 1) * cap, :] = dtin[k, pl.ds(pl.multiple_of((me ^ r) * cap, cap), cap), :]

    def zp(h, k):
        return rc(zs.at[h, k], zr.at[h, k], zp_s.at[h, k], zp_r.at[h, k], zpeer(k))

    def combine_chunk(h):
        for r in range(1, 8):
            ret(h, r).wait_recv()
        for k in (2, 3, 1):
            zs[h, k] = tn(dtp[k], rbuf[h, k]).astype(BF16)
            zp(h, k).start()
        own[h] = tn(dtp[0], rbuf[h, 0])

    second(0)
    for h in range(4):
        combine_chunk(h)
    for k in range(1, 4):
        second(k)
    for k in range(4):
        third(k)

    for k in range(4):
        for t in range(2):
            for r in (0, X, Y, X ^ Y):
                got(t, k, r ^ CORE)

    docs_eye = lax.broadcasted_iota(jnp.int32, (docs, docs), 0) == lax.broadcasted_iota(jnp.int32, (docs, docs), 1)
    length = jnp.sum(jnp.where(docs_eye, length_ref[...].astype(F32), 0.0), axis=1, keepdims=True)
    scale = float(128 * slots) / length
    kc = factor_ref.shape[1]
    for w in range(4):
        block = fac_all[w, 0 : w + 1].reshape(-1, kc)
        total[:, w * kc : (w + 1) * kc] = nn(noise_ref[:, 0 : block.shape[0]], block)

    def final_chunk(h, _):
        for k in range(1, 4):
            zp(h, k).wait_recv()
        summed = own[h]
        for k in range(1, 4):
            summed = summed + zr[h, k].astype(F32)
        value = summed * scale + bias_ref[h]
        hidden = (jnp.maximum(value, 0.0) + jnp.log1p(jnp.exp(-jnp.abs(value)))).astype(BF16)
        total[...] += nt(hidden, head_all[h].reshape(-1, hc))
        return 0

    lax.fori_loop(0, 4, final_chunk, 0)

    for k in range(1, 4):
        zc(k).wait_send()
        zd(k).wait_send()
        for t, c in enumerate(zw(k)):
            guarded(t, z <= v, c.wait_send)
    for r in range(1, 8):
        for c in pc(r):
            c.wait_send()
    for k in range(4):
        for t in range(2):
            first, then = turn(t, k)
            sent(t, k, 0, X)
            sent(t, k, 0, Y)
            sent(t, k, first, then)
            for r in (0, X, Y, X ^ Y):
                sent(t, k, r, CORE)

    def drain(h, _):
        for r in range(1, 8):
            ret(h, r).wait_send()
        for k in range(1, 4):
            zp(h, k).wait_send()
        return 0

    lax.fori_loop(0, 4, drain, 0)


def fused(
    counts, doc_owner, doc_sub, doc_len, first_weight, first_bias, head_weight, head_bias, factor, noise_draw
):
    docs, slots, width = counts.shape
    hidden = first_weight.shape[1]
    cap = 2 * docs * slots // 32
    hc, topics = head_weight.shape[0], head_bias.shape[0]
    rows = 8 * cap
    dma = pltpu.SemaphoreType.DMA
    kd, kc = head_weight.shape[1], factor.shape[0]
    total = pl.pallas_call(
        functools.partial(kernel, cap),
        out_shape=jax.ShapeDtypeStruct((docs, topics), F32),
        in_specs=[pl.BlockSpec(memory_space=pltpu.VMEM)] * 9,
        out_specs=pl.BlockSpec(memory_space=pltpu.VMEM),
        scratch_shapes=[
            pltpu.VMEM((4, rows + 16, width), BF16),
            pltpu.VMEM((4, rows, docs), BF16),
            pltpu.VMEM((4, rows + 16, width), BF16),
            pltpu.VMEM((4, rows, docs), BF16),
            pltpu.VMEM((8, 4, cap, width), BF16),
            pltpu.VMEM((8, 4, 16, 128), BF16),
            pltpu.VMEM((8, 4 * cap, 8 * width), BF16),
            pltpu.VMEM((4, 8, 4, cap, hc), BF16),
            pltpu.VMEM((4, 4, rows, hc), BF16),
            pltpu.VMEM((4, 4, docs, hc), BF16),
            pltpu.VMEM((4, 4, docs, hc), BF16),
            pltpu.VMEM((4, docs, hc), F32),
            pltpu.VMEM((4, rows, docs), BF16),
            pltpu.VMEM((4, 4, 2, kd, hc), BF16),
            pltpu.VMEM((4, 4, 2, factor.shape[1], kc), BF16),
            pltpu.VMEM((docs * slots, width), F32),
            dma((4,)), dma((4,)), dma((4,)), dma((4,)), dma((2, 4)), dma((2, 4)),
            dma((8,)), dma((8,)), dma((8,)), dma((8,)),
            dma((4, 8)), dma((4, 8)), dma((4, 4)), dma((4, 4)),
            dma((2, 4, 8)), dma((2, 4, 8)),
        ],
        compiler_params=pltpu.CompilerParams(
            collective_id=0, has_side_effects=True, vmem_limit_bytes=58 * 1024 * 1024
        ),
    )(
        counts.reshape(docs * slots, width),
        doc_owner.T,
        doc_sub.T,
        doc_len.reshape(1, docs),
        first_weight,
        first_bias.reshape(4, 1, hc),
        head_weight.T,
        factor.T,
        noise_draw,
    )
    return (total + head_bias).astype(BF16)


def local(
    counts,
    doc_owner,
    doc_sub,
    doc_len,
    first_weight,
    first_bias,
    head_weight,
    head_bias,
    factor,
    noise_draw,
):
    vocab_devices = lax.axis_size("vocab")
    docs_devices = lax.axis_size("docs")
    device_count = vocab_devices * docs_devices
    docs_here, slot_count, block_width = counts.shape
    hidden_width = first_weight.shape[1]
    per_owner = first_weight.shape[0] // block_width
    capacity = max(2, 2 * docs_here * slot_count // device_count)
    owner_flat = doc_owner.reshape(-1)
    onehot = (owner_flat[:, None] == jnp.arange(device_count, dtype=jnp.int32)[None, :]).astype(
        jnp.int32
    )
    position = jnp.sum(jnp.cumsum(onehot, axis=0) * onehot, axis=1) - 1
    slot_index = owner_flat * capacity + position
    flat_rows = counts.reshape(-1, block_width)
    send_rows = (
        jnp.zeros((device_count * capacity, block_width), counts.dtype)
        .at[slot_index]
        .set(flat_rows)
    )
    send_sub = (
        jnp.zeros((device_count * capacity,), jnp.bfloat16)
        .at[slot_index]
        .set(doc_sub.reshape(-1).astype(jnp.bfloat16))
    )
    send_rows = send_rows.reshape(vocab_devices, docs_devices, capacity, block_width)
    send_sub = send_sub.reshape(vocab_devices, docs_devices, capacity)
    got_rows, got_sub = (
        lax.all_to_all(
            lax.all_to_all(send_rows, "vocab", split_axis=0, concat_axis=0, tiled=True),
            "docs",
            split_axis=1,
            concat_axis=1,
            tiled=True,
        ),
        lax.all_to_all(
            lax.all_to_all(send_sub, "vocab", split_axis=0, concat_axis=0, tiled=True),
            "docs",
            split_axis=1,
            concat_axis=1,
            tiled=True,
        ),
    )
    got_rows = got_rows.reshape(-1, block_width)
    got_sub = got_sub.reshape(-1).astype(jnp.int32)
    select = (got_sub[:, None] == jnp.arange(per_owner, dtype=jnp.int32)[None, :]).astype(
        jnp.bfloat16
    )
    spread = (select[:, :, None] * got_rows[:, None, :]).reshape(-1, per_owner * block_width)
    owner_terms = jnp.dot(spread, first_weight, preferred_element_type=jnp.float32).astype(
        jnp.bfloat16
    )
    owner_terms = owner_terms.reshape(vocab_devices, docs_devices, capacity, hidden_width)
    returned = lax.all_to_all(
        lax.all_to_all(owner_terms, "vocab", split_axis=0, concat_axis=0, tiled=True),
        "docs",
        split_axis=1,
        concat_axis=1,
        tiled=True,
    )
    returned = returned.reshape(-1, hidden_width)
    own_rows = returned[slot_index].reshape(docs_here, slot_count, hidden_width).astype(jnp.float32)
    summed = jnp.sum(own_rows, axis=1)
    length_scale = 128.0 * slot_count / doc_len.astype(jnp.float32)
    hidden = jax.nn.softplus(summed * length_scale[:, None] + first_bias).astype(jnp.bfloat16)
    panel_rows = lax.all_gather(head_weight, "docs", axis=1, tiled=True)
    location = jnp.dot(
        hidden,
        lax.all_gather(panel_rows, "vocab", axis=0, tiled=True),
        preferred_element_type=jnp.float32,
    )
    factor_panel = lax.all_gather(factor, "docs", axis=1, tiled=True)
    correlated = lax.dot_general(
        noise_draw,
        lax.all_gather(factor_panel, "vocab", axis=0, tiled=True),
        (((1,), (1,)), ((), ())),
        preferred_element_type=jnp.float32,
    )
    return (location + head_bias + correlated).astype(jnp.bfloat16)


def solution(mesh):
    small = mesh.shape["vocab"] == 4 and mesh.shape["docs"] == 8
    return jax.shard_map(
        fused if small else local,
        mesh=mesh,
        in_specs=(
            P(("vocab", "docs"), None, None),
            P(("vocab", "docs"), None),
            P(("vocab", "docs"), None),
            P(("vocab", "docs")),
            P(("vocab", "docs"), None),
            P(),
            P("vocab", "docs"),
            P(),
            P("vocab", "docs"),
            P(("vocab", "docs"), None),
        ),
        out_specs=P(("vocab", "docs"), None),
        check_vma=False,
    )
```

```python
import functools

import jax
import jax.numpy as jnp
from jax import lax
from jax.experimental import pallas as pl
from jax.experimental.pallas import tpu as pltpu
from jax.sharding import PartitionSpec as P

MESH = pl.DeviceIdType.MESH
F32 = jnp.float32
BF16 = jnp.bfloat16
X, Y, CORE = 1, 4, 2
ORDER = (5, 7, 1, 3, 4, 6, 2)


def nt(a, b):
    return lax.dot_general(a, b, (((1,), (1,)), ((), ())), preferred_element_type=F32)


def tn(a, b):
    return lax.dot_general(a, b, (((0,), (0,)), ((), ())), preferred_element_type=F32)


def nn(a, b):
    return jnp.dot(a, b, preferred_element_type=F32)


def kernel(
    cap,
    counts_ref, owner_ref, sub_ref, length_ref, weight_ref, bias_ref,
    head_ref, factor_ref, noise_ref,
    total,
    cbuf, dtbuf, zin, dtin, pin, pmeta, spread, obuf, rbuf, zs, zr, own, dtp,
    head_all, fac_all, wide, hid,
    zc_s, zc_r, zd_s, zd_r, zw_s, zw_r, pc_s, pc_r, pm_s, pm_r,
    ret_s, ret_r, zp_s, zp_r, wp_s, wp_r,
):
    slots, docs = owner_ref.shape
    width = counts_ref.shape[1]
    owners = 32
    rows = 8 * cap
    hc = head_ref.shape[1]
    v = lax.axis_index("vocab")
    d = lax.axis_index("docs")
    z = d // 2
    x = d % 2
    me = v * 2 + x

    def zpeer(k):
        return (v, (z ^ k) * 2 + x)

    def ppeer(r):
        j = me ^ r
        return (j // 2, z * 2 + j % 2)

    def rc(src, dst, s, r, dev):
        return pltpu.make_async_remote_copy(
            src_ref=src, dst_ref=dst, send_sem=s, recv_sem=r, device_id=dev, device_id_type=MESH
        )

    barrier = pltpu.get_barrier_semaphore()
    for k in range(1, 4):
        pl.semaphore_signal(barrier, inc=1, device_id=zpeer(k), device_id_type=MESH)
    for r in range(1, 8):
        pl.semaphore_signal(barrier, inc=1, device_id=ppeer(r), device_id_type=MESH)

    upper = jnp.where(
        lax.broadcasted_iota(jnp.int32, (docs, docs), 0)
        <= lax.broadcasted_iota(jnp.int32, (docs, docs), 1), 1.0, 0.0
    ).astype(BF16)
    owner_iota = lax.broadcasted_iota(jnp.int32, (owners, docs), 0)
    meta_iota = lax.broadcasted_iota(jnp.int32, (64, docs), 0)
    place_iota = lax.broadcasted_iota(jnp.int32, (128, docs), 0)
    row_iota = lax.broadcasted_iota(jnp.int32, (rows, docs), 0)
    carry = jnp.zeros((owners, 1), F32)
    wide[...] = counts_ref[...].astype(F32)
    counts = [wide[pl.ds(s, docs, stride=slots), :].astype(BF16) for s in range(slots)]
    meta = jnp.zeros((64, 128), F32)
    full = []
    for s in range(slots):
        o = owner_ref[s : s + 1, :]
        hot = jnp.where(owner_iota == o, 1.0, 0.0)
        cum = nn(hot.astype(BF16), upper) + carry
        carry = carry + jnp.sum(hot, axis=1, keepdims=True)
        pos = (jnp.sum(hot * cum, axis=0, keepdims=True) - 1.0).astype(jnp.int32)
        oz = (o >> 1) & 3
        oi = (o >> 3) * 2 + (o & 1)
        full.append(oz * rows + oi * cap + pos)
        named = jnp.where(
            meta_iota == oz * 16 + oi, jnp.broadcast_to(sub_ref[s : s + 1, :], (64, docs)).astype(F32), 0.0
        ).astype(BF16)
        placed = jnp.where(place_iota == pos, 1.0, 0.0).astype(BF16)
        meta = meta + nt(named, placed)
    for zo in range(4):
        acc = jnp.zeros((rows, width), F32)
        dt = jnp.zeros((rows, docs), F32)
        for s in range(slots):
            sel = jnp.where(row_iota + zo * rows == full[s], 1.0, 0.0)
            acc = acc + nn(sel.astype(BF16), counts[s])
            dt = dt + sel
        cbuf[zo, 0:rows, :] = acc.astype(BF16)
        cbuf[zo, rows : rows + 16, :] = meta[zo * 16 : zo * 16 + 16, :].astype(BF16)
        dtbuf[zo] = dt.astype(BF16)

    pl.semaphore_wait(barrier, 10)

    def zc(k):
        return rc(cbuf.at[z ^ k], zin.at[k], zc_s.at[k], zc_r.at[k], zpeer(k))

    def zd(k):
        return rc(dtbuf.at[z ^ k], dtin.at[k], zd_s.at[k], zd_r.at[k], zpeer(k))

    def zw(k):
        return (
            rc(head_ref, head_all.at[v, z, x], zw_s.at[0, k], zw_r.at[0, k], zpeer(k)),
            rc(factor_ref, fac_all.at[v, z, x], zw_s.at[1, k], zw_r.at[1, k], zpeer(k)),
        )

    def piece(t, k, r, hop):
        j = me ^ r
        ref = (head_all, fac_all)[t].at[j // 2, z ^ k, j % 2]
        rel = r ^ hop
        return rc(ref, ref, wp_s.at[t, k, rel], wp_r.at[t, k, rel], ppeer(hop or CORE))

    def guarded(t, held, act):
        if t:
            pl.when(held)(act)
        else:
            act()

    def go(t, k, r, hop):
        guarded(t, (z ^ k) <= (me ^ r) // 2, lambda: piece(t, k, r, hop).start())

    def sent(t, k, r, hop):
        guarded(t, (z ^ k) <= (me ^ r) // 2, lambda: piece(t, k, r, hop).wait_send())

    def got(t, k, rel):
        guarded(t, (z ^ k) <= (me ^ rel) // 2, lambda: piece(t, k, rel, 0).wait_recv())

    def turn(t, k):
        return (Y, X) if t or k == 3 else (X, Y)

    head_all[v, z, x] = head_ref[...]
    fac_all[v, z, x] = factor_ref[...]
    for k in (2, 3, 1):
        zc(k).start()
    zin[0] = cbuf[z]
    dtin[0] = dtbuf[z]

    def pc(r):
        j = me ^ r
        return (
            rc(zin.at[:, pl.ds(pl.multiple_of(j * cap, cap), cap), :], pin.at[r], pc_s.at[r], pc_r.at[r], ppeer(r)),
            rc(zin.at[:, pl.ds(rows, 16), :], pmeta.at[r], pm_s.at[r], pm_r.at[r], ppeer(r)),
        )

    for k in range(1, 4):
        zc(k).wait_recv()
    for r in ORDER:
        for c in pc(r):
            c.start()
    for k in (2, 3, 1):
        for t, c in enumerate(zw(k)):
            guarded(t, z <= v, c.start)
    for k in (2, 3, 1):
        zd(k).start()
    for t in range(2):
        for hop in (X, Y, CORE):
            go(t, 0, 0, hop)
    pin[0] = zin[:, pl.ds(pl.multiple_of(me * cap, cap), cap), :]
    pmeta[0] = zin[:, rows : rows + 16, :]

    ones = jnp.ones((128, 128), BF16)
    pick = lax.broadcasted_iota(jnp.int32, (16, 128), 0) == me
    eye = lax.broadcasted_iota(jnp.int32, (cap, 128), 0) == lax.broadcasted_iota(jnp.int32, (cap, 128), 1)

    def spread_one(r, _):
        for k in range(4):
            line = jnp.sum(jnp.where(pick, pmeta[r, k].astype(F32), 0.0), axis=0, keepdims=True)
            sub = nn(jnp.where(eye, line, 0.0).astype(BF16), ones)
            got = pin[r, k].astype(F32)
            for b in range(8):
                spread[r, k * cap : (k + 1) * cap, b * width : (b + 1) * width] = jnp.where(
                    sub == float(b), got, 0.0
                ).astype(BF16)
        return 0

    spread_one(0, 0)
    for r in ORDER:
        for c in pc(r):
            c.wait_recv()
    lax.fori_loop(1, 8, spread_one, 0)

    def ret(h, r):
        return rc(
            obuf.at[h, r], rbuf.at[h, :, pl.ds(r * cap, cap), :], ret_s.at[h, r], ret_r.at[h, r], ppeer(r)
        )

    def owner_chunk(h, _):
        cols = weight_ref[:, pl.ds(pl.multiple_of(h * hc, hc), hc)]
        for pair in ((5, 7), (1, 3), (4, 6), (2, 0)):
            for r in pair:
                got = nn(spread[r], cols).astype(BF16).reshape(4, cap, hc)
                if r:
                    obuf[h, r] = got
                    ret(h, r).start()
                else:
                    rbuf[h, :, 0:cap, :] = got
        return 0

    lax.fori_loop(0, 4, owner_chunk, 0)

    for k in range(1, 4):
        for t, c in enumerate(zw(k)):
            guarded(t, (z ^ k) <= v, c.wait_recv)
            for hop in (X, Y, CORE):
                go(t, k, 0, hop)

    def second(k):
        for t in range(2):
            first, then = turn(t, k)
            got(t, k, first)
            go(t, k, first, then)
            go(t, k, first, CORE)
            got(t, k, then)
            go(t, k, then, CORE)

    def third(k):
        for t in range(2):
            got(t, k, X ^ Y)
            go(t, k, X ^ Y, CORE)

    for k in range(1, 4):
        zd(k).wait_recv()
    for k in range(4):
        for r in range(8):
            dtp[k, r * cap : (r + 1) * cap, :] = dtin[k, pl.ds(pl.multiple_of((me ^ r) * cap, cap), cap), :]

    def zp(h, k):
        return rc(zs.at[h, k], zr.at[h, k], zp_s.at[h, k], zp_r.at[h, k], zpeer(k))

    def combine_chunk(h):
        for r in range(1, 8):
            ret(h, r).wait_recv()
        for k in (2, 3, 1):
            zs[h, k] = tn(dtp[k], rbuf[h, k]).astype(BF16)
            zp(h, k).start()
        own[h] = tn(dtp[0], rbuf[h, 0])

    second(0)
    for h in range(4):
        combine_chunk(h)
    for k in range(1, 4):
        second(k)
    for k in range(4):
        third(k)

    docs_eye = lax.broadcasted_iota(jnp.int32, (docs, docs), 0) == lax.broadcasted_iota(jnp.int32, (docs, docs), 1)
    length = jnp.sum(jnp.where(docs_eye, length_ref[...].astype(F32), 0.0), axis=1, keepdims=True)
    scale = float(128 * slots) / length
    def hidden_chunk(h, _):
        for k in range(1, 4):
            zp(h, k).wait_recv()
        summed = own[h]
        for k in range(1, 4):
            summed = summed + zr[h, k].astype(F32)
        value = summed * scale + bias_ref[h]
        hid[h] = (jnp.maximum(value, 0.0) + jnp.log1p(jnp.exp(-jnp.abs(value)))).astype(BF16)
        return 0

    lax.fori_loop(0, 4, hidden_chunk, 0)

    for t in (1, 0):
        for k in range(4):
            for r in (0, X, Y, X ^ Y):
                got(t, k, r ^ CORE)
        if t:
            kc = factor_ref.shape[1]
            for w in range(4):
                block = fac_all[w, 0 : w + 1].reshape(-1, kc)
                total[:, w * kc : (w + 1) * kc] = nn(noise_ref[:, 0 : block.shape[0]], block)

    def location_chunk(h, _):
        total[...] += nt(hid[h], head_all[h].reshape(-1, hc))
        return 0

    lax.fori_loop(0, 4, location_chunk, 0)

    for k in range(1, 4):
        zc(k).wait_send()
        zd(k).wait_send()
        for t, c in enumerate(zw(k)):
            guarded(t, z <= v, c.wait_send)
    for r in range(1, 8):
        for c in pc(r):
            c.wait_send()
    for k in range(4):
        for t in range(2):
            first, then = turn(t, k)
            sent(t, k, 0, X)
            sent(t, k, 0, Y)
            sent(t, k, first, then)
            for r in (0, X, Y, X ^ Y):
                sent(t, k, r, CORE)

    def drain(h, _):
        for r in range(1, 8):
            ret(h, r).wait_send()
        for k in range(1, 4):
            zp(h, k).wait_send()
        return 0

    lax.fori_loop(0, 4, drain, 0)


def fused(
    counts, doc_owner, doc_sub, doc_len, first_weight, first_bias, head_weight, head_bias, factor, noise_draw
):
    docs, slots, width = counts.shape
    hidden = first_weight.shape[1]
    cap = 2 * docs * slots // 32
    hc, topics = head_weight.shape[0], head_bias.shape[0]
    rows = 8 * cap
    dma = pltpu.SemaphoreType.DMA
    kd, kc = head_weight.shape[1], factor.shape[0]
    total = pl.pallas_call(
        functools.partial(kernel, cap),
        out_shape=jax.ShapeDtypeStruct((docs, topics), F32),
        in_specs=[pl.BlockSpec(memory_space=pltpu.VMEM)] * 9,
        out_specs=pl.BlockSpec(memory_space=pltpu.VMEM),
        scratch_shapes=[
            pltpu.VMEM((4, rows + 16, width), BF16),
            pltpu.VMEM((4, rows, docs), BF16),
            pltpu.VMEM((4, rows + 16, width), BF16),
            pltpu.VMEM((4, rows, docs), BF16),
            pltpu.VMEM((8, 4, cap, width), BF16),
            pltpu.VMEM((8, 4, 16, 128), BF16),
            pltpu.VMEM((8, 4 * cap, 8 * width), BF16),
            pltpu.VMEM((4, 8, 4, cap, hc), BF16),
            pltpu.VMEM((4, 4, rows, hc), BF16),
            pltpu.VMEM((4, 4, docs, hc), BF16),
            pltpu.VMEM((4, 4, docs, hc), BF16),
            pltpu.VMEM((4, docs, hc), F32),
            pltpu.VMEM((4, rows, docs), BF16),
            pltpu.VMEM((4, 4, 2, kd, hc), BF16),
            pltpu.VMEM((4, 4, 2, factor.shape[1], kc), BF16),
            pltpu.VMEM((docs * slots, width), F32),
            pltpu.VMEM((4, docs, hc), BF16),
            dma((4,)), dma((4,)), dma((4,)), dma((4,)), dma((2, 4)), dma((2, 4)),
            dma((8,)), dma((8,)), dma((8,)), dma((8,)),
            dma((4, 8)), dma((4, 8)), dma((4, 4)), dma((4, 4)),
            dma((2, 4, 8)), dma((2, 4, 8)),
        ],
        compiler_params=pltpu.CompilerParams(
            collective_id=0, has_side_effects=True, vmem_limit_bytes=58 * 1024 * 1024
        ),
    )(
        counts.reshape(docs * slots, width),
        doc_owner.T,
        doc_sub.T,
        doc_len.reshape(1, docs),
        first_weight,
        first_bias.reshape(4, 1, hc),
        head_weight.T,
        factor.T,
        noise_draw,
    )
    return (total + head_bias).astype(BF16)


def local(
    counts,
    doc_owner,
    doc_sub,
    doc_len,
    first_weight,
    first_bias,
    head_weight,
    head_bias,
    factor,
    noise_draw,
):
    vocab_devices = lax.axis_size("vocab")
    docs_devices = lax.axis_size("docs")
    device_count = vocab_devices * docs_devices
    docs_here, slot_count, block_width = counts.shape
    hidden_width = first_weight.shape[1]
    per_owner = first_weight.shape[0] // block_width
    capacity = max(2, 2 * docs_here * slot_count // device_count)
    owner_flat = doc_owner.reshape(-1)
    onehot = (owner_flat[:, None] == jnp.arange(device_count, dtype=jnp.int32)[None, :]).astype(
        jnp.int32
    )
    position = jnp.sum(jnp.cumsum(onehot, axis=0) * onehot, axis=1) - 1
    slot_index = owner_flat * capacity + position
    flat_rows = counts.reshape(-1, block_width)
    send_rows = (
        jnp.zeros((device_count * capacity, block_width), counts.dtype)
        .at[slot_index]
        .set(flat_rows)
    )
    send_sub = (
        jnp.zeros((device_count * capacity,), jnp.bfloat16)
        .at[slot_index]
        .set(doc_sub.reshape(-1).astype(jnp.bfloat16))
    )
    send_rows = send_rows.reshape(vocab_devices, docs_devices, capacity, block_width)
    send_sub = send_sub.reshape(vocab_devices, docs_devices, capacity)
    got_rows, got_sub = (
        lax.all_to_all(
            lax.all_to_all(send_rows, "vocab", split_axis=0, concat_axis=0, tiled=True),
            "docs",
            split_axis=1,
            concat_axis=1,
            tiled=True,
        ),
        lax.all_to_all(
            lax.all_to_all(send_sub, "vocab", split_axis=0, concat_axis=0, tiled=True),
            "docs",
            split_axis=1,
            concat_axis=1,
            tiled=True,
        ),
    )
    got_rows = got_rows.reshape(-1, block_width)
    got_sub = got_sub.reshape(-1).astype(jnp.int32)
    select = (got_sub[:, None] == jnp.arange(per_owner, dtype=jnp.int32)[None, :]).astype(
        jnp.bfloat16
    )
    spread = (select[:, :, None] * got_rows[:, None, :]).reshape(-1, per_owner * block_width)
    owner_terms = jnp.dot(spread, first_weight, preferred_element_type=jnp.float32).astype(
        jnp.bfloat16
    )
    owner_terms = owner_terms.reshape(vocab_devices, docs_devices, capacity, hidden_width)
    returned = lax.all_to_all(
        lax.all_to_all(owner_terms, "vocab", split_axis=0, concat_axis=0, tiled=True),
        "docs",
        split_axis=1,
        concat_axis=1,
        tiled=True,
    )
    returned = returned.reshape(-1, hidden_width)
    own_rows = returned[slot_index].reshape(docs_here, slot_count, hidden_width).astype(jnp.float32)
    summed = jnp.sum(own_rows, axis=1)
    length_scale = 128.0 * slot_count / doc_len.astype(jnp.float32)
    hidden = jax.nn.softplus(summed * length_scale[:, None] + first_bias).astype(jnp.bfloat16)
    panel_rows = lax.all_gather(head_weight, "docs", axis=1, tiled=True)
    location = jnp.dot(
        hidden,
        lax.all_gather(panel_rows, "vocab", axis=0, tiled=True),
        preferred_element_type=jnp.float32,
    )
    factor_panel = lax.all_gather(factor, "docs", axis=1, tiled=True)
    correlated = lax.dot_general(
        noise_draw,
        lax.all_gather(factor_panel, "vocab", axis=0, tiled=True),
        (((1,), (1,)), ((), ())),
        preferred_element_type=jnp.float32,
    )
    return (location + head_bias + correlated).astype(jnp.bfloat16)


def solution(mesh):
    small = mesh.shape["vocab"] == 4 and mesh.shape["docs"] == 8
    return jax.shard_map(
        fused if small else local,
        mesh=mesh,
        in_specs=(
            P(("vocab", "docs"), None, None),
            P(("vocab", "docs"), None),
            P(("vocab", "docs"), None),
            P(("vocab", "docs")),
            P(("vocab", "docs"), None),
            P(),
            P("vocab", "docs"),
            P(),
            P("vocab", "docs"),
            P(("vocab", "docs"), None),
        ),
        out_specs=P(("vocab", "docs"), None),
        check_vma=False,
    )
```
